32 devices in a mesh: tm: 4 (over z), space: 8 (over y, x, core).
Axes of the slice: x: 2, y: 2, z: 4, core: 2. Of those that a mesh axis runs over, the one named last changes fastest.
Arguments:
- snaps: bfloat16 [4096, 3, 16384], P('tm', None, 'space')
- phase_bin: int32 [4096], P('tm'), may hold values from 0 to 15, as said below
- owner_order: int32 [16], replicated, may hold values from 0 to 15, each once
- modes: bfloat16 [16, 128, 3, 16384], P(None, None, None, 'space'), may hold values from -0.02734375 to 0.02734375
Outputs:
- phase_mean: bfloat16 [16, 3, 16384], P('tm', None, 'space')
- coefficients: float32 [4096, 128], P('tm')
The draws below stay inside these ranges and needn't reach their ends.
Inputs may be any that keep to these rules, and one draw needn't show every extreme that they name: `phase_bin`: every bin is named by at least one snapshot; in each aligned block of 1024 snapshots no bin is named more than 128 times.
All inputs are finite; a program needn't handle non-finite values.
Results may differ from the reference program's by a relative error of at most 0.0068.
Values may be sent and summed in bfloat16 or wider, within the bound.
A program may use at most 192 MiB of HBM per device.

```python
import jax
import jax.numpy as jnp
from jax import lax

NBINS = 16
MODES = 128
COMP = 3
T_DEV = 1024
T_SNAP = 4096
CELLS = 16384


def bins_helper(key):
    steps = jnp.arange(T_SNAP, dtype=jnp.int32)
    local = steps % T_DEV
    block = steps // T_DEV
    start = jax.random.randint(jax.random.fold_in(key, 21), (), 0, NBINS).astype(jnp.int32)
    heavy = (start + block) % NBINS
    cls = local // 2 % NBINS
    jitter = jax.random.randint(jax.random.fold_in(key, 11), (T_SNAP,), 0, 3).astype(jnp.int32)
    jitter = jnp.where(cls == heavy, 0, jitter)
    jitter = jnp.where(cls == (heavy + NBINS - 1) % NBINS, 1, jitter)
    jitter = jnp.where(cls == (heavy + NBINS - 2) % NBINS, 2, jitter)
    return (local // 2 + jitter * (local % 2)) % NBINS


def draw_phase_bin(key, part):
    return bins_helper(key)


def draw_snaps(key, part):
    bins_now = bins_helper(key)
    pattern = jax.random.normal(jax.random.fold_in(key, 12), (NBINS, COMP, CELLS), jnp.float32)
    noise = jax.random.normal(jax.random.fold_in(key, 13), (T_SNAP, COMP, CELLS), jnp.float32)
    return (2.0 * pattern[bins_now] + noise).astype(jnp.bfloat16)


def level_of(stream_key, extent, split, low, high):
    loudness = 1.0
    for axis_at, parts in split:
        heights = jax.random.uniform(jax.random.fold_in(jax.random.fold_in(stream_key, 6), axis_at), (parts,), jnp.float32, low / len(split), high / len(split))
        loudness = loudness * jnp.repeat(jnp.exp(heights), extent[axis_at] // parts).reshape((-1,) + (1,) * (len(extent) - 1 - axis_at))
    return loudness


def centred(stream_key, extent, deviation, limit, split=(), kind=jnp.bfloat16):
    drawn = jax.random.normal(stream_key, extent, jnp.float32) * deviation
    if len(split) > 0:
        drawn = level_of(stream_key, extent, split, -0.22, 0.18) * drawn
    return jnp.clip(drawn, min=-limit, max=limit).astype(kind)


def setup_inputs(seed: int = 0) -> dict:
    splits = jax.random.split(jax.random.key(seed), 5)
    snaps = draw_snaps(jax.random.fold_in(splits[4], 71), 0)
    phase_bin = draw_phase_bin(jax.random.fold_in(splits[4], 71), 0)
    owner_order = jax.random.permutation(splits[2], NBINS).astype(jnp.int32)
    modes = centred(splits[3], (NBINS, MODES, COMP, CELLS), (COMP * CELLS) ** -0.5, 0.02734375, ((3, 8),))
    return {"snaps": snaps, "phase_bin": phase_bin, "owner_order": owner_order, "modes": modes}


def reference(snaps, phase_bin, owner_order, modes):
    flattened = snaps.reshape(T_SNAP, COMP * CELLS)
    bin_ids = jnp.arange(NBINS, dtype=jnp.int32)
    onehot = (phase_bin[None, :] == bin_ids[:, None])
    bin_sum = jnp.dot(onehot.astype(jnp.bfloat16), flattened, preferred_element_type=jnp.float32)
    bin_count = jnp.sum(onehot.astype(jnp.float32), axis=1)
    bin_mean = (bin_sum / bin_count[:, None]).astype(jnp.bfloat16)
    phase_mean = bin_mean[owner_order].reshape(NBINS, COMP, CELLS)
    fluct = (flattened.astype(jnp.float32) - bin_mean[phase_bin].astype(jnp.float32)).astype(jnp.bfloat16)
    modes_flat = modes.reshape(NBINS, MODES, COMP * CELLS)
    fluct_blocks = fluct.reshape(T_SNAP // 8, 8, COMP * CELLS)
    bin_blocks = phase_bin.reshape(T_SNAP // 8, 8)

    def one_block(pair):
        block_rows, block_bins = pair
        chosen = modes_flat[block_bins].astype(jnp.float32)
        return jnp.einsum("tk,tmk->tm", block_rows.astype(jnp.float32), chosen)

    coefficients = lax.map(one_block, (fluct_blocks, bin_blocks)).reshape(T_SNAP, MODES)
    return phase_mean, coefficients
```

```python
import functools

import jax
import jax.numpy as jnp
from jax import lax
from jax.experimental import pallas as pl
from jax.experimental.pallas import tpu as pltpu
from jax.sharding import PartitionSpec as P

MESH = pl.DeviceIdType.MESH
F32 = jnp.float32
BF16 = jnp.bfloat16
I32 = jnp.int32
NT = (((1,), (1,)), ((), ()))
CHUNK = 256
TILE = 16
CAP = 128


def slots_of(rows):
    chunks = rows // CHUNK
    return TILE * ((2 * CAP + (TILE - 2) * chunks) // TILE + chunks)


def iota(shape, dim):
    return lax.broadcasted_iota(I32, shape, dim)


def ones_where(cond):
    return jnp.where(cond, 1.0, 0.0)


def owners(ownrow, rank_of_row):
    bins = ownrow.shape[1]
    mat = jnp.broadcast_to(ownrow[...].astype(F32), (bins, bins))
    return jnp.sum(jnp.where(rank_of_row == iota((bins, bins), 1), mat, 0.0), axis=1, keepdims=True).astype(I32)


def plan(tm, binrow, ownrow, slotv, table_out, keyv):
    bins, rows = ownrow.shape[1], binrow.shape[1]
    pairs, chunks, tiles = bins // 2, rows // CHUNK, CHUNK // TILE
    slots = slots_of(rows)
    own_rows = bins // tm

    hot = jnp.concatenate(
        [ones_where(binrow[:, k * CHUNK:(k + 1) * CHUNK] == iota((bins, CHUNK), 0)) for k in range(chunks)], 0)
    groups = chunks * bins
    before = ones_where(iota((CHUNK, CHUNK), 0) < iota((CHUNK, CHUNK), 1)).astype(BF16)
    rank = jnp.dot(hot.astype(BF16), before, preferred_element_type=F32)
    count = jnp.broadcast_to(jnp.sum(hot, axis=1, keepdims=True), (groups, 128)).astype(BF16)
    gi, gj = iota((groups, groups), 0), iota((groups, groups), 1)
    lower = ones_where((gj < gi) & (gj // bins == gi // bins)).astype(BF16)
    base = jnp.dot(lower, count, preferred_element_type=F32)
    hi, hj = iota((chunks * pairs, groups), 0), iota((chunks * pairs, groups), 1)
    pair_count = jnp.dot(ones_where(hj // 2 == hi).astype(BF16), count, preferred_element_type=F32).astype(I32)
    pair_base = jnp.dot(
        ones_where(hj == 2 * hi).astype(BF16), base.astype(BF16), preferred_element_type=F32).astype(I32)
    first = pair_base // TILE
    n_tiles = jnp.where(pair_count > 0, (pair_base + pair_count - 1) // TILE - first + 1, 0)
    place = iota((pairs, 128), 1)
    skip = jnp.zeros((pairs, 128), I32)
    table = jnp.zeros((pairs, 128), I32)
    own = owners(ownrow, iota((bins, bins), 0))
    for k in range(chunks):
        bk = binrow[:, k * CHUNK:(k + 1) * CHUNK]
        here = slice(k * bins, (k + 1) * bins)
        f, nk = first[k * pairs:(k + 1) * pairs], n_tiles[k * pairs:(k + 1) * pairs]
        table = table + jnp.where((place >= skip) & (place < skip + nk), tiles * k + f + place - skip, 0)
        slot = jnp.sum(hot[here] * (base[here][:, 0:1] + rank[here]), axis=0, keepdims=True)
        in_pair = ones_where(bk // 2 == iota((pairs, CHUNK), 0))
        shift = jnp.sum(in_pair * (TILE * (skip - f)).astype(F32)[:, 0:1], axis=0, keepdims=True)
        keyv[0:1, k * CHUNK:(k + 1) * CHUNK] = (slot + shift).astype(I32) + bk * slots
        by_owner = ones_where(bk == own)
        j = iota((bins, CHUNK), 0)
        row = (8 * (j // own_rows) + j % own_rows).astype(F32)
        keyv[1:2, k * CHUNK:(k + 1) * CHUNK] = jnp.sum(by_owner * row, axis=0, keepdims=True).astype(I32)
        slotv[:, k * CHUNK:(k + 1) * CHUNK] = slot.astype(I32)
        skip = skip + nk
    table_out[...] = table


def kernel(
    tm, space, binrow, slotrow, ownrow, ownsm, tbl, key, snaps, modes, coef_out, mean_out,
    X, Xs, mo, perm, prods, sums, ssend, rsum, cnt, rcnt, mean, mj,
    acc, sendc, rsc, agc,
    xsem, msem, s_sum, r_sum, s_cnt, r_cnt, s_mj, r_mj, s_rs, r_rs, s_ag, r_ag,
):
    comp, rows, cells = snaps.shape
    bins, nm = modes.shape[0], modes.shape[2]
    pairs, chunks, tiles = bins // 2, rows // CHUNK, CHUNK // TILE
    slots = slots_of(rows)
    own_rows = bins // tm
    w = cells // tm
    blk = rows // space
    me_t = lax.axis_index("tm")
    me_s = lax.axis_index("space")

    xcopies = [
        [pltpu.make_async_copy(
            snaps.at[c, pl.ds(k * CHUNK, CHUNK)], X.at[c, pl.ds(k * CHUNK, CHUNK)], xsem.at[c, k])
         for k in range(chunks)] for c in range(comp)]
    for line in xcopies:
        for cp in line:
            cp.start()

    barrier = pltpu.get_barrier_semaphore()
    for d in range(1, tm):
        pl.semaphore_signal(barrier, inc=1, device_id={"tm": lax.rem(me_t + d, tm)}, device_id_type=MESH)
    for d in range(1, space):
        pl.semaphore_signal(barrier, inc=1, device_id={"space": lax.rem(me_s + d, space)}, device_id_type=MESH)

    own = owners(ownrow, iota((bins, bins), 0))
    for k in range(chunks):
        sl = slice(k * CHUNK, (k + 1) * CHUNK)
        perm[k, :CHUNK, :] = ones_where(slotrow[:, sl] == iota((CHUNK, CHUNK), 0)).astype(BF16)
        perm[k, CHUNK:, :] = ones_where(binrow[:, sl] == own).astype(BF16)
    for q in range(tm):
        mine = owners(ownrow, q * own_rows + iota((bins, bins), 0) % own_rows)
        cnt[q] = jnp.broadcast_to(
            jnp.sum(ones_where(mine == binrow[...]), axis=1, keepdims=True), (bins, 128))

    def fetch(b):
        return pltpu.make_async_copy(
            modes.at[b], mo.at[:, b], msem.at[b])

    tm_copies = []

    def to_owners(src, dst, send, recv, *at):
        for d in range(1, tm):
            q = lax.rem(me_t + d, tm)
            a = pltpu.make_async_remote_copy(
                src_ref=src.at[(q,) + at], dst_ref=dst.at[(d - 1,) + at], send_sem=send.at[(d - 1,) + at],
                recv_sem=recv.at[(d - 1,) + at], device_id={"tm": q}, device_id_type=MESH)
            a.start()
            tm_copies.append(a)

    for c in range(comp):
        for k in range(chunks):
            xcopies[c][k].wait()
            if c == comp - 2 and k == chunks // 2:
                fetch(0).start()
                fetch(1).start()
            if c == comp - 1 and k == chunks // 2:
                for b in range(2, bins):
                    fetch(b).start()
            for n in range(tm):
                sl = slice(n * w, (n + 1) * w)
                y = jnp.dot(perm[k], X[c, k * CHUNK:(k + 1) * CHUNK, sl], preferred_element_type=F32)
                Xs[c, k * tiles:(k + 1) * tiles, :, sl] = y[:CHUNK].astype(BF16).reshape(tiles, TILE, w)
                part = y[CHUNK:]
                if k > 0:
                    part = part + sums[n]
                if k < chunks - 1:
                    sums[n] = part
                else:
                    for q in range(tm):
                        ssend[q, c, n * own_rows:(n + 1) * own_rows, :] = part[q * own_rows:(q + 1) * own_rows]
        if c == 0:
            pl.semaphore_wait(barrier, tm - 1 + space - 1)
            to_owners(cnt, rcnt, s_cnt, r_cnt)
        to_owners(ssend, rsum, s_sum, r_sum, c)

    def project(p):
        prod = jnp.zeros((slots, 2 * nm), F32)
        for c in range(comp):
            sorted_rows = jnp.concatenate([Xs[c, tbl[p, s]] for s in range(slots // TILE)], 0)
            prod += lax.dot_general(sorted_rows, mo[c, pl.ds(2 * p, 2)].reshape(2 * nm, cells), NT, preferred_element_type=F32)
        for b in range(2):
            prods[pl.ds(pl.multiple_of((2 * p + b) * slots, TILE), slots)] = prod[:, b * nm:(b + 1) * nm]

    def early(p, _):
        fetch(2 * p).wait()
        fetch(2 * p + 1).wait()
        project(p)
        return 0

    def later(p, _):
        project(p)
        return 0

    split = pairs - 2
    lax.fori_loop(0, split, early, 0)
    for b in range(2 * split, bins):
        fetch(b).wait()

    for cp in tm_copies:
        cp.wait()
    total_cnt = cnt[me_t]
    for d in range(tm - 1):
        total_cnt = total_cnt + rcnt[d]
    for c in range(comp):
        tot = ssend[me_t, c]
        for d in range(tm - 1):
            tot = tot + rsum[d, c]
        m = tot / total_cnt[:, 0:1]
        mean[c] = m.astype(BF16)
        for n in range(tm):
            mean_out[c, :, n * w:(n + 1) * w] = m[n * own_rows:(n + 1) * own_rows].astype(BF16)
    at = [ownsm[0, me_t * own_rows + i] for i in range(own_rows)]
    tall = (own_rows * nm, bins)
    picked = jnp.zeros(tall, F32)
    for n in range(tm):
        p = jnp.zeros(tall, F32)
        for c in range(comp):
            lhs = jnp.concatenate([mo[c, a, :, n * w:(n + 1) * w] for a in at], 0)
            p += lax.dot_general(lhs, mean[c], NT, preferred_element_type=F32)
        picked += jnp.where(iota(tall, 1) == n * own_rows + iota(tall, 0) // nm, p, 0.0)
    flat = picked[:nm]
    for i in range(1, own_rows):
        flat = flat + picked[i * nm:(i + 1) * nm]
    flat = flat.T
    mine = flat[:own_rows]
    for n in range(1, tm):
        mine = mine + flat[n * own_rows:(n + 1) * own_rows]
    mj[pl.ds(pl.multiple_of(me_t * 8, 8), 8)] = jnp.concatenate(
        [mine, jnp.zeros((8 - own_rows, nm), F32)], 0)

    def mj_copy(d, q):
        return pltpu.make_async_remote_copy(
            src_ref=mj.at[pl.ds(pl.multiple_of(q * 8, 8), 8)], dst_ref=mj.at[pl.ds(pl.multiple_of(q * 8, 8), 8)],
            send_sem=s_mj.at[d - 1], recv_sem=r_mj.at[d - 1],
            device_id={"tm": lax.rem(me_t + d, tm)}, device_id_type=MESH)

    for d in range(1, tm):
        mj_copy(d, me_t).start()

    lax.fori_loop(split, pairs, later, 0)

    for d in range(1, tm):
        mj_copy(d, me_t).wait_send()
        mj_copy(d, lax.rem(me_t + tm - d, tm)).wait_recv()

    def block(s):
        return pl.ds(pl.multiple_of(s * blk, blk), blk)

    def unsorted(q):
        def some(i, _):
            for r in range(TILE):
                t = q * blk + i * TILE + r
                acc[pl.ds(i * TILE + r, 1)] = prods[pl.ds(key[0, t], 1)] - mj[pl.ds(key[1, t], 1)]
            return 0

        lax.fori_loop(0, blk // TILE, some, 0)
        return acc[...]

    rs_copies = []
    for d in range(1, space):
        q = lax.rem(me_s + d, space)
        sendc[d - 1] = unsorted(q).astype(BF16)
        a = pltpu.make_async_remote_copy(
            src_ref=sendc.at[d - 1], dst_ref=rsc.at[d - 1], send_sem=s_rs.at[d - 1],
            recv_sem=r_rs.at[d - 1], device_id={"space": q}, device_id_type=MESH)
        a.start()
        rs_copies.append(a)
    tot = unsorted(me_s)
    for d in range(space - 1):
        rs_copies[d].wait()
        tot = tot + rsc[d].astype(F32)
    mine = block(me_s)
    agc[mine, :] = tot.astype(BF16)
    ag_copies = []
    for d in range(1, space):
        a = pltpu.make_async_remote_copy(
            src_ref=agc.at[mine], dst_ref=agc.at[mine], send_sem=s_ag.at[d - 1],
            recv_sem=r_ag.at[d - 1], device_id={"space": lax.rem(me_s + d, space)}, device_id_type=MESH)
        a.start()
        ag_copies.append(a)
    for d in range(1, space):
        ag_copies[d - 1].wait_send()
        src = block(lax.rem(me_s + space - d, space))
        pltpu.make_async_remote_copy(
            src_ref=agc.at[src], dst_ref=agc.at[src], send_sem=s_ag.at[d - 1],
            recv_sem=r_ag.at[d - 1], device_id={"space": lax.rem(me_s + d, space)}, device_id_type=MESH).wait_recv()
    coef_out[...] = agc[...]


def on_device(snaps, phase_bin, owner_order, modes):
    rows, comp, cells = snaps.shape
    bins, nm = modes.shape[0], modes.shape[1]
    tm, space = lax.axis_size("tm"), lax.axis_size("space")
    blk, w, own_rows = rows // space, cells // tm, bins // tm
    chunks, slots = rows // CHUNK, slots_of(rows)
    ownrow = owner_order.reshape(1, bins)
    vm = pl.BlockSpec(memory_space=pltpu.VMEM)
    sm = pl.BlockSpec(memory_space=pltpu.SMEM)
    hbm = pl.BlockSpec(memory_space=pl.ANY)
    dma = pltpu.SemaphoreType.DMA
    binrow = phase_bin.reshape(1, rows)
    slotrow, table, key = pl.pallas_call(
        functools.partial(plan, tm),
        out_shape=(
            jax.ShapeDtypeStruct((1, rows), I32),
            jax.ShapeDtypeStruct((bins // 2, 128), I32),
            jax.ShapeDtypeStruct((2, rows), I32),
        ),
        in_specs=[vm, vm],
        out_specs=(vm, vm, vm),
    )(binrow, ownrow)
    coef, mean = pl.pallas_call(
        functools.partial(kernel, tm, space),
        out_shape=(
            jax.ShapeDtypeStruct((rows, nm), BF16),
            jax.ShapeDtypeStruct((comp, own_rows, cells), BF16),
        ),
        in_specs=[vm, vm, vm, sm, sm, sm, hbm, hbm],
        out_specs=(vm, vm),
        scratch_shapes=[
            pltpu.VMEM((comp, rows, cells), BF16),
            pltpu.VMEM((comp, rows // TILE, TILE, cells), BF16),
            pltpu.VMEM((comp, bins, nm, cells), BF16),
            pltpu.VMEM((chunks, CHUNK + bins, CHUNK), BF16),
            pltpu.VMEM((bins * slots, nm), F32),
            pltpu.VMEM((tm, bins, w), F32),
            pltpu.VMEM((tm, comp, bins, w), F32),
            pltpu.VMEM((tm - 1, comp, bins, w), F32),
            pltpu.VMEM((tm, bins, 128), F32),
            pltpu.VMEM((tm - 1, bins, 128), F32),
            pltpu.VMEM((comp, bins, w), BF16),
            pltpu.VMEM((tm * 8, nm), F32),
            pltpu.VMEM((blk, nm), F32),
            pltpu.VMEM((space - 1, blk, nm), BF16),
            pltpu.VMEM((space - 1, blk, nm), BF16),
            pltpu.VMEM((rows, nm), BF16),
            dma((comp, chunks)), dma((bins,)),
            dma((tm - 1, comp)), dma((tm - 1, comp)), dma((tm - 1,)), dma((tm - 1,)), dma((tm - 1,)), dma((tm - 1,)),
            dma((space - 1,)), dma((space - 1,)), dma((space - 1,)), dma((space - 1,)),
        ],
        compiler_params=pltpu.CompilerParams(
            collective_id=0, has_side_effects=True, vmem_limit_bytes=61 * 1024 * 1024
        ),
        cost_estimate=pl.CostEstimate(
            flops=2 * slots * bins * nm * comp * cells,
            bytes_accessed=2 * comp * cells * (rows + bins * nm), transcendentals=0),
    )(binrow, slotrow, ownrow, ownrow, table, key, snaps.transpose(1, 0, 2), modes.transpose(0, 2, 1, 3))
    return mean.transpose(1, 0, 2), coef.astype(F32)


def solution(mesh):
    in_specs = (P("tm", None, "space"), P("tm"), P(), P(None, None, None, "space"))
    out_specs = (P("tm", None, "space"), P("tm", None))
    return jax.shard_map(
        on_device, mesh=mesh, in_specs=in_specs, out_specs=out_specs, check_vma=False
    )
```

```python
import functools

import jax
import jax.numpy as jnp
from jax import lax
from jax.experimental import pallas as pl
from jax.experimental.pallas import tpu as pltpu
from jax.sharding import PartitionSpec as P

MESH = pl.DeviceIdType.MESH
F32 = jnp.float32
BF16 = jnp.bfloat16
I32 = jnp.int32
NT = (((1,), (1,)), ((), ()))
CHUNK = 256
TILE = 16
BIN, SLOT, KEY, MEAN, TABLE, OWNER = range(6)
UNROLL = 32
HALVES = 2
CAP = 128


def slots_of(rows):
    chunks = rows // CHUNK
    return TILE * ((2 * CAP + (TILE - 2) * chunks) // TILE + chunks)


def iota(shape, dim):
    return lax.broadcasted_iota(I32, shape, dim)


def ones_where(cond):
    return jnp.where(cond, 1.0, 0.0)


def owners(ownrow, rank_of_row):
    bins = ownrow.shape[1]
    mat = jnp.broadcast_to(ownrow.astype(F32), (bins, bins))
    return jnp.sum(jnp.where(rank_of_row == iota((bins, bins), 1), mat, 0.0), axis=1, keepdims=True).astype(I32)


def plan(tm, binrow, ownrow, meta):
    bins, rows = ownrow.shape[1], binrow.shape[1]
    pairs, chunks, tiles = bins // 2, rows // CHUNK, CHUNK // TILE
    slots = slots_of(rows)
    own_rows = bins // tm

    hot = jnp.concatenate(
        [ones_where(binrow[:, k * CHUNK:(k + 1) * CHUNK] == iota((bins, CHUNK), 0)) for k in range(chunks)], 0)
    groups = chunks * bins
    before = ones_where(iota((CHUNK, CHUNK), 0) < iota((CHUNK, CHUNK), 1)).astype(BF16)
    rank = jnp.dot(hot.astype(BF16), before, preferred_element_type=F32)
    count = jnp.broadcast_to(jnp.sum(hot, axis=1, keepdims=True), (groups, 128)).astype(BF16)
    gi, gj = iota((groups, groups), 0), iota((groups, groups), 1)
    lower = ones_where((gj < gi) & (gj // bins == gi // bins)).astype(BF16)
    base = jnp.dot(lower, count, preferred_element_type=F32)
    hi, hj = iota((chunks * pairs, groups), 0), iota((chunks * pairs, groups), 1)
    pair_count = jnp.dot(ones_where(hj // 2 == hi).astype(BF16), count, preferred_element_type=F32).astype(I32)
    pair_base = jnp.dot(
        ones_where(hj == 2 * hi).astype(BF16), base.astype(BF16), preferred_element_type=F32).astype(I32)
    first = pair_base // TILE
    n_tiles = jnp.where(pair_count > 0, (pair_base + pair_count - 1) // TILE - first + 1, 0)
    place = iota((pairs, 128), 1)
    skip = jnp.zeros((pairs, 128), I32)
    table = jnp.zeros((pairs, 128), I32)
    own = owners(ownrow[...], iota((bins, bins), 0))
    for k in range(chunks):
        bk = binrow[:, k * CHUNK:(k + 1) * CHUNK]
        here = slice(k * bins, (k + 1) * bins)
        f, nk = first[k * pairs:(k + 1) * pairs], n_tiles[k * pairs:(k + 1) * pairs]
        table = table + jnp.where((place >= skip) & (place < skip + nk), tiles * k + f + place - skip, 0)
        slot = jnp.sum(hot[here] * (base[here][:, 0:1] + rank[here]), axis=0, keepdims=True)
        in_pair = ones_where(bk // 2 == iota((pairs, CHUNK), 0))
        shift = jnp.sum(in_pair * (TILE * (skip - f)).astype(F32)[:, 0:1], axis=0, keepdims=True)
        meta[KEY:KEY + 1, k * CHUNK:(k + 1) * CHUNK] = (slot + shift).astype(I32) + bk * slots
        by_owner = ones_where(bk == own)
        j = iota((bins, CHUNK), 0)
        row = (8 * (j // own_rows) + j % own_rows).astype(F32)
        meta[MEAN:MEAN + 1, k * CHUNK:(k + 1) * CHUNK] = jnp.sum(by_owner * row, axis=0, keepdims=True).astype(I32)
        meta[SLOT:SLOT + 1, k * CHUNK:(k + 1) * CHUNK] = slot.astype(I32)
        meta[BIN:BIN + 1, k * CHUNK:(k + 1) * CHUNK] = bk
        skip = skip + nk
    for p in range(pairs):
        meta[TABLE:TABLE + 1, p * 128:(p + 1) * 128] = table[p:p + 1]
    meta[OWNER:OWNER + 1, 0:bins] = ownrow[...]


def kernel(
    tm, space, meta, snaps, modes, coef_out, mean_out,
    metav, metas, meanv, X, Xs, mo, perm, prods, sums, ssend, rsum, cnt, rcnt, mean, mj,
    acc, sendc, rsc, agc,
    vsem, ssem, osem, osem_c, xsem, msem, s_sum, r_sum, s_cnt, r_cnt, s_mj, r_mj, s_rs, r_rs, s_ag, r_ag,
):
    comp, rows, cells = snaps.shape
    bins, nm = modes.shape[0], modes.shape[2]
    pairs, chunks, tiles = bins // 2, rows // CHUNK, CHUNK // TILE
    slots = slots_of(rows)
    own_rows = bins // tm
    w = cells // tm
    blk = rows // space
    me_t = lax.axis_index("tm")
    me_s = lax.axis_index("space")

    xcopies = [
        [pltpu.make_async_copy(
            snaps.at[c, pl.ds(k * CHUNK, CHUNK)], X.at[c, pl.ds(k * CHUNK, CHUNK)], xsem.at[c, k])
         for k in range(chunks)] for c in range(comp)]
    for line in xcopies:
        for cp in line:
            cp.start()

    vcopy = pltpu.make_async_copy(meta, metav, vsem)
    scopy = pltpu.make_async_copy(meta, metas, ssem)
    vcopy.start()
    scopy.start()

    barrier = pltpu.get_barrier_semaphore()
    for d in range(1, tm):
        pl.semaphore_signal(barrier, inc=1, device_id={"tm": lax.rem(me_t + d, tm)}, device_id_type=MESH)
    for d in range(1, space):
        pl.semaphore_signal(barrier, inc=1, device_id={"space": lax.rem(me_s + d, space)}, device_id_type=MESH)

    vcopy.wait()
    binrow, slotrow = metav[BIN:BIN + 1], metav[SLOT:SLOT + 1]
    ownrow = metav[OWNER:OWNER + 1, :bins]
    own = owners(ownrow, iota((bins, bins), 0))
    for k in range(chunks):
        sl = slice(k * CHUNK, (k + 1) * CHUNK)
        perm[k, :CHUNK, :] = ones_where(slotrow[:, sl] == iota((CHUNK, CHUNK), 0)).astype(BF16)
        perm[k, CHUNK:, :] = ones_where(binrow[:, sl] == own).astype(BF16)
    for q in range(tm):
        mine = owners(ownrow, q * own_rows + iota((bins, bins), 0) % own_rows)
        cnt[q] = jnp.broadcast_to(
            jnp.sum(ones_where(mine == binrow), axis=1, keepdims=True), (bins, 128))

    def fetch(b):
        return pltpu.make_async_copy(
            modes.at[b], mo.at[:, b], msem.at[b])

    tm_copies = []

    def to_owners(src, dst, send, recv, *at):
        for d in range(1, tm):
            q = lax.rem(me_t + d, tm)
            a = pltpu.make_async_remote_copy(
                src_ref=src.at[(q,) + at], dst_ref=dst.at[(d - 1,) + at], send_sem=send.at[(d - 1,) + at],
                recv_sem=recv.at[(d - 1,) + at], device_id={"tm": q}, device_id_type=MESH)
            a.start()
            tm_copies.append(a)

    for c in range(comp):
        for k in range(chunks):
            xcopies[c][k].wait()
            if c == comp - 2 and k == chunks // 2:
                fetch(0).start()
                fetch(1).start()
            if c == comp - 1 and k == chunks // 2:
                for b in range(2, bins):
                    fetch(b).start()
            for n in range(tm):
                sl = slice(n * w, (n + 1) * w)
                y = jnp.dot(perm[k], X[c, k * CHUNK:(k + 1) * CHUNK, sl], preferred_element_type=F32)
                Xs[c, k * tiles:(k + 1) * tiles, :, sl] = y[:CHUNK].astype(BF16).reshape(tiles, TILE, w)
                part = y[CHUNK:]
                if k > 0:
                    part = part + sums[n]
                if k < chunks - 1:
                    sums[n] = part
                else:
                    for q in range(tm):
                        ssend[q, c, n * own_rows:(n + 1) * own_rows, :] = part[q * own_rows:(q + 1) * own_rows]
        if c == 1:
            pl.semaphore_wait(barrier, tm - 1 + space - 1)
            to_owners(ssend, rsum, s_sum, r_sum, 0)
            to_owners(cnt, rcnt, s_cnt, r_cnt)
        if c >= 1:
            to_owners(ssend, rsum, s_sum, r_sum, c)

    scopy.wait()

    def project(p):
        prod = jnp.zeros((slots, 2 * nm), F32)
        for c in range(comp):
            sorted_rows = jnp.concatenate([Xs[c, metas[TABLE, p * 128 + s]] for s in range(slots // TILE)], 0)
            prod += lax.dot_general(sorted_rows, mo[c, pl.ds(2 * p, 2)].reshape(2 * nm, cells), NT, preferred_element_type=F32)
        for b in range(2):
            prods[pl.ds(pl.multiple_of((2 * p + b) * slots, TILE), slots)] = prod[:, b * nm:(b + 1) * nm]

    def early(p, _):
        fetch(2 * p).wait()
        fetch(2 * p + 1).wait()
        project(p)
        return 0

    def later(p, _):
        project(p)
        return 0

    split = pairs - 3
    lax.fori_loop(0, split, early, 0)
    for b in range(2 * split, bins):
        fetch(b).wait()

    for cp in tm_copies:
        cp.wait()
    total_cnt = cnt[me_t]
    for d in range(tm - 1):
        total_cnt = total_cnt + rcnt[d]
    for c in range(comp):
        tot = ssend[me_t, c]
        for d in range(tm - 1):
            tot = tot + rsum[d, c]
        m = tot / total_cnt[:, 0:1]
        mean[c] = m.astype(BF16)
        for n in range(tm):
            meanv[c, :, n * w:(n + 1) * w] = m[n * own_rows:(n + 1) * own_rows].astype(BF16)
    ocopy = pltpu.make_async_copy(meanv, mean_out, osem)
    ocopy.start()
    at = [metas[OWNER, me_t * own_rows + i] for i in range(own_rows)]
    tall = (own_rows * nm, bins)
    picked = jnp.zeros(tall, F32)
    for n in range(tm):
        p = jnp.zeros(tall, F32)
        for c in range(comp):
            lhs = jnp.concatenate([mo[c, a, :, n * w:(n + 1) * w] for a in at], 0)
            p += lax.dot_general(lhs, mean[c], NT, preferred_element_type=F32)
        picked += jnp.where(iota(tall, 1) == n * own_rows + iota(tall, 0) // nm, p, 0.0)
    flat = picked[:nm]
    for i in range(1, own_rows):
        flat = flat + picked[i * nm:(i + 1) * nm]
    flat = flat.T
    mine = flat[:own_rows]
    for n in range(1, tm):
        mine = mine + flat[n * own_rows:(n + 1) * own_rows]
    mj[pl.ds(pl.multiple_of(me_t * 8, 8), 8)] = jnp.concatenate(
        [mine, jnp.zeros((8 - own_rows, nm), F32)], 0)

    def mj_copy(d, q):
        return pltpu.make_async_remote_copy(
            src_ref=mj.at[pl.ds(pl.multiple_of(q * 8, 8), 8)], dst_ref=mj.at[pl.ds(pl.multiple_of(q * 8, 8), 8)],
            send_sem=s_mj.at[d - 1], recv_sem=r_mj.at[d - 1],
            device_id={"tm": lax.rem(me_t + d, tm)}, device_id_type=MESH)

    for d in range(1, tm):
        mj_copy(d, me_t).start()

    lax.fori_loop(split, pairs, later, 0)

    for d in range(1, tm):
        mj_copy(d, me_t).wait_send()
        mj_copy(d, lax.rem(me_t + tm - d, tm)).wait_recv()

    part = blk // HALVES

    def rows_at(s, h):
        return s * blk + h * part

    def unsorted(q, h):
        def some(i, _):
            for r in range(UNROLL):
                t = rows_at(q, h) + i * UNROLL + r
                acc[h, pl.ds(i * UNROLL + r, 1)] = (
                    prods[pl.ds(metas[KEY, t], 1)] - mj[pl.ds(metas[MEAN, t], 1)])
            return 0

        lax.fori_loop(0, part // UNROLL, some, 0)

    rs_copies = []
    for h in range(HALVES):
        for d in range(1, space):
            q = lax.rem(me_s + d, space)
            unsorted(q, h)
            sendc[h, d - 1] = acc[h].astype(BF16)
            a = pltpu.make_async_remote_copy(
                src_ref=sendc.at[h, d - 1], dst_ref=rsc.at[h, d - 1], send_sem=s_rs.at[h, d - 1],
                recv_sem=r_rs.at[h, d - 1], device_id={"space": q}, device_id_type=MESH)
            a.start()
            rs_copies.append(a)
        unsorted(me_s, h)

    def slab(s, h):
        return coef_out.at[pl.ds(pl.multiple_of(rows_at(s, h), TILE), part)]

    waits = []
    for h in range(HALVES):
        tot = acc[h]
        for d in range(space - 1):
            rs_copies[h * (space - 1) + d].wait()
            tot = tot + rsc[h, d].astype(F32)
        agc[h] = tot.astype(BF16)
        for d in range(1, space):
            a = pltpu.make_async_remote_copy(
                src_ref=agc.at[h], dst_ref=slab(me_s, h), send_sem=s_ag.at[h, d - 1],
                recv_sem=r_ag.at[h, d - 1], device_id={"space": lax.rem(me_s + d, space)}, device_id_type=MESH)
            a.start()
            waits.append(a.wait_send)
            waits.append(pltpu.make_async_remote_copy(
                src_ref=agc.at[h], dst_ref=slab(lax.rem(me_s + space - d, space), h), send_sem=s_ag.at[h, d - 1],
                recv_sem=r_ag.at[h, d - 1], device_id={"space": lax.rem(me_s + d, space)},
                device_id_type=MESH).wait_recv)
        a = pltpu.make_async_copy(agc.at[h], slab(me_s, h), osem_c.at[h])
        a.start()
        waits.append(a.wait)
    ocopy.wait()
    for wait in waits:
        wait()


def finish(coef, mean, coef_out, mean_out, sem):
    copy = pltpu.make_async_copy(mean, mean_out, sem)
    copy.start()
    coef_out[...] = coef[...].astype(F32)
    copy.wait()


def on_device(snaps, phase_bin, owner_order, modes):
    rows, comp, cells = snaps.shape
    bins, nm = modes.shape[0], modes.shape[1]
    tm, space = lax.axis_size("tm"), lax.axis_size("space")
    blk, w, own_rows = rows // space, cells // tm, bins // tm
    chunks, slots = rows // CHUNK, slots_of(rows)
    ownrow = owner_order.reshape(1, bins)
    vm = pl.BlockSpec(memory_space=pltpu.VMEM)
    hbm = pl.BlockSpec(memory_space=pl.ANY)
    dma = pltpu.SemaphoreType.DMA
    binrow = phase_bin.reshape(1, rows)
    meta = pl.pallas_call(
        functools.partial(plan, tm),
        out_shape=jax.ShapeDtypeStruct((8, rows), I32),
        in_specs=[vm, vm],
        out_specs=vm,
    )(binrow, ownrow)
    coef, mean = pl.pallas_call(
        functools.partial(kernel, tm, space),
        out_shape=(
            jax.ShapeDtypeStruct((rows, nm), BF16),
            jax.ShapeDtypeStruct((comp, own_rows, cells), BF16),
        ),
        in_specs=[hbm, hbm, hbm],
        out_specs=(hbm, hbm),
        scratch_shapes=[
            pltpu.VMEM((8, rows), I32),
            pltpu.SMEM((8, rows), I32),
            pltpu.VMEM((comp, own_rows, cells), BF16),
            pltpu.VMEM((comp, rows, cells), BF16),
            pltpu.VMEM((comp, rows // TILE, TILE, cells), BF16),
            pltpu.VMEM((comp, bins, nm, cells), BF16),
            pltpu.VMEM((chunks, CHUNK + bins, CHUNK), BF16),
            pltpu.VMEM((bins * slots, nm), F32),
            pltpu.VMEM((tm, bins, w), F32),
            pltpu.VMEM((tm, comp, bins, w), F32),
            pltpu.VMEM((tm - 1, comp, bins, w), F32),
            pltpu.VMEM((tm, bins, 128), F32),
            pltpu.VMEM((tm - 1, bins, 128), F32),
            pltpu.VMEM((comp, bins, w), BF16),
            pltpu.VMEM((tm * 8, nm), F32),
            pltpu.VMEM((HALVES, blk // HALVES, nm), F32),
            pltpu.VMEM((HALVES, space - 1, blk // HALVES, nm), BF16),
            pltpu.VMEM((HALVES, space - 1, blk // HALVES, nm), BF16),
            pltpu.VMEM((HALVES, blk // HALVES, nm), BF16),
            dma(()), dma(()), dma(()), dma((HALVES,)), dma((comp, chunks)), dma((bins,)),
            dma((tm - 1, comp)), dma((tm - 1, comp)), dma((tm - 1,)), dma((tm - 1,)), dma((tm - 1,)), dma((tm - 1,)),
            dma((HALVES, space - 1)), dma((HALVES, space - 1)), dma((HALVES, space - 1)), dma((HALVES, space - 1)),
        ],
        compiler_params=pltpu.CompilerParams(
            collective_id=0, has_side_effects=True, vmem_limit_bytes=61 * 1024 * 1024
        ),
        cost_estimate=pl.CostEstimate(
            flops=2 * slots * bins * nm * comp * cells,
            bytes_accessed=2 * comp * cells * (rows + bins * nm), transcendentals=0),
    )(meta, snaps.transpose(1, 0, 2), modes.transpose(0, 2, 1, 3))
    coef, mean = pl.pallas_call(
        finish,
        out_shape=(
            jax.ShapeDtypeStruct((rows, nm), F32),
            jax.ShapeDtypeStruct((comp, own_rows, cells), BF16),
        ),
        in_specs=[vm, hbm],
        out_specs=(vm, hbm),
        scratch_shapes=[dma(())],
    )(coef, mean)
    return mean.transpose(1, 0, 2), coef


def solution(mesh):
    in_specs = (P("tm", None, "space"), P("tm"), P(), P(None, None, None, "space"))
    out_specs = (P("tm", None, "space"), P("tm", None))
    return jax.shard_map(
        on_device, mesh=mesh, in_specs=in_specs, out_specs=out_specs, check_vma=False
    )
```

```python
import functools

import jax
import jax.numpy as jnp
from jax import lax
from jax.experimental import pallas as pl
from jax.experimental.pallas import tpu as pltpu
from jax.sharding import PartitionSpec as P

MESH = pl.DeviceIdType.MESH
F32 = jnp.float32
BF16 = jnp.bfloat16
I32 = jnp.int32
NT = (((1,), (1,)), ((), ()))
CHUNK = 256
TILE = 16
BIN, SLOT, KEY, MEAN, TABLE, OWNER = range(6)
UNROLL = 32
HALVES = 2
CAP = 128


def slots_of(rows):
    chunks = rows // CHUNK
    return TILE * ((2 * CAP + (TILE - 2) * chunks) // TILE + chunks)


def iota(shape, dim):
    return lax.broadcasted_iota(I32, shape, dim)


def ones_where(cond):
    return jnp.where(cond, 1.0, 0.0)


def owners(ownrow, rank_of_row):
    bins = ownrow.shape[1]
    mat = jnp.broadcast_to(ownrow.astype(F32), (bins, bins))
    return jnp.sum(jnp.where(rank_of_row == iota((bins, bins), 1), mat, 0.0), axis=1, keepdims=True).astype(I32)


def plan(tm, binrow, ownrow, meta):
    bins, rows = ownrow.shape[1], binrow.shape[1]
    pairs, chunks, tiles = bins // 2, rows // CHUNK, CHUNK // TILE
    slots = slots_of(rows)
    own_rows = bins // tm

    hot = jnp.concatenate(
        [ones_where(binrow[:, k * CHUNK:(k + 1) * CHUNK] == iota((bins, CHUNK), 0)) for k in range(chunks)], 0)
    groups = chunks * bins
    before = ones_where(iota((CHUNK, CHUNK), 0) < iota((CHUNK, CHUNK), 1)).astype(BF16)
    rank = jnp.dot(hot.astype(BF16), before, preferred_element_type=F32)
    count = jnp.broadcast_to(jnp.sum(hot, axis=1, keepdims=True), (groups, 128)).astype(BF16)
    gi, gj = iota((groups, groups), 0), iota((groups, groups), 1)
    lower = ones_where((gj < gi) & (gj // bins == gi // bins)).astype(BF16)
    base = jnp.dot(lower, count, preferred_element_type=F32)
    hi, hj = iota((chunks * pairs, groups), 0), iota((chunks * pairs, groups), 1)
    pair_count = jnp.dot(ones_where(hj // 2 == hi).astype(BF16), count, preferred_element_type=F32).astype(I32)
    pair_base = jnp.dot(
        ones_where(hj == 2 * hi).astype(BF16), base.astype(BF16), preferred_element_type=F32).astype(I32)
    first = pair_base // TILE
    n_tiles = jnp.where(pair_count > 0, (pair_base + pair_count - 1) // TILE - first + 1, 0)
    place = iota((pairs, 128), 1)
    skip = jnp.zeros((pairs, 128), I32)
    table = jnp.zeros((pairs, 128), I32)
    own = owners(ownrow[...], iota((bins, bins), 0))
    for k in range(chunks):
        bk = binrow[:, k * CHUNK:(k + 1) * CHUNK]
        here = slice(k * bins, (k + 1) * bins)
        f, nk = first[k * pairs:(k + 1) * pairs], n_tiles[k * pairs:(k + 1) * pairs]
        table = table + jnp.where((place >= skip) & (place < skip + nk), tiles * k + f + place - skip, 0)
        slot = jnp.sum(hot[here] * (base[here][:, 0:1] + rank[here]), axis=0, keepdims=True)
        in_pair = ones_where(bk // 2 == iota((pairs, CHUNK), 0))
        shift = jnp.sum(in_pair * (TILE * (skip - f)).astype(F32)[:, 0:1], axis=0, keepdims=True)
        meta[KEY:KEY + 1, k * CHUNK:(k + 1) * CHUNK] = (slot + shift).astype(I32) + bk * slots
        by_owner = ones_where(bk == own)
        j = iota((bins, CHUNK), 0)
        row = (8 * (j // own_rows) + j % own_rows).astype(F32)
        meta[MEAN:MEAN + 1, k * CHUNK:(k + 1) * CHUNK] = jnp.sum(by_owner * row, axis=0, keepdims=True).astype(I32)
        meta[SLOT:SLOT + 1, k * CHUNK:(k + 1) * CHUNK] = slot.astype(I32)
        meta[BIN:BIN + 1, k * CHUNK:(k + 1) * CHUNK] = bk
        skip = skip + nk
    for p in range(pairs):
        meta[TABLE:TABLE + 1, p * 128:(p + 1) * 128] = table[p:p + 1]
    meta[OWNER:OWNER + 1, 0:bins] = ownrow[...]


def kernel(
    tm, space, meta, snaps, modes, coef_out, mean_out,
    metav, metas, meanv, X, Xs, mo, perm, prods, sums, ssend, rsum, cnt, rcnt, mean, mj,
    byrow, fix, acc, sendc, rsc, agc,
    vsem, ssem, osem, osem_c, xsem, msem, s_sum, r_sum, s_cnt, r_cnt, s_mj, r_mj, s_rs, r_rs, s_ag, r_ag,
):
    comp, rows, cells = snaps.shape
    bins, nm = modes.shape[0], modes.shape[2]
    pairs, chunks, tiles = bins // 2, rows // CHUNK, CHUNK // TILE
    slots = slots_of(rows)
    own_rows = bins // tm
    w = cells // tm
    blk = rows // space
    part = blk // HALVES
    mj_rows = 8 * tm
    me_t = lax.axis_index("tm")
    me_s = lax.axis_index("space")

    def every(n, f, first=0):
        lax.fori_loop(first, n, lambda i, _: (f(i), 0)[1], 0)

    vcopy = pltpu.make_async_copy(meta, metav, vsem)
    scopy = pltpu.make_async_copy(meta, metas, ssem)
    vcopy.start()
    scopy.start()

    def rows_in(c, k):
        sl = pl.ds(pl.multiple_of(k * CHUNK, CHUNK), CHUNK)
        return pltpu.make_async_copy(snaps.at[c, sl], X.at[c, sl], xsem.at[c, k])

    every(comp * chunks, lambda i: rows_in(i // chunks, i % chunks).start())

    def fetch(b):
        return pltpu.make_async_copy(modes.at[b], mo.at[:, b], msem.at[b])

    every(bins, lambda b: fetch(b).start())

    barrier = pltpu.get_barrier_semaphore()
    for d in range(1, tm):
        pl.semaphore_signal(barrier, inc=1, device_id={"tm": lax.rem(me_t + d, tm)}, device_id_type=MESH)
    for d in range(1, space):
        pl.semaphore_signal(barrier, inc=1, device_id={"space": lax.rem(me_s + d, space)}, device_id_type=MESH)

    vcopy.wait()
    binrow, slotrow = metav[BIN:BIN + 1], metav[SLOT:SLOT + 1]
    ownrow = metav[OWNER:OWNER + 1, :bins]
    own = owners(ownrow, iota((bins, bins), 0))
    for k in range(chunks):
        sl = slice(k * CHUNK, (k + 1) * CHUNK)
        perm[k, :CHUNK, :] = ones_where(slotrow[:, sl] == iota((CHUNK, CHUNK), 0)).astype(BF16)
        perm[k, CHUNK:, :] = ones_where(binrow[:, sl] == own).astype(BF16)
    for q in range(tm):
        mine = owners(ownrow, q * own_rows + iota((bins, bins), 0) % own_rows)
        cnt[q] = jnp.broadcast_to(
            jnp.sum(ones_where(mine == binrow), axis=1, keepdims=True), (bins, 128))
    for k in range(rows // 128):
        sl = slice(k * 128, (k + 1) * 128)
        at_row = jnp.broadcast_to(metav[MEAN:MEAN + 1, sl], (128, 128)).T
        byrow[sl, :] = ones_where(iota((128, 128), 1) == at_row).astype(BF16)

    def sum_copy(c, d):
        q = lax.rem(me_t + d, tm)
        return pltpu.make_async_remote_copy(
            src_ref=ssend.at[q, c], dst_ref=rsum.at[d - 1, c], send_sem=s_sum.at[d - 1, c],
            recv_sem=r_sum.at[d - 1, c], device_id={"tm": q}, device_id_type=MESH)

    def cnt_copy(d):
        q = lax.rem(me_t + d, tm)
        return pltpu.make_async_remote_copy(
            src_ref=cnt.at[q], dst_ref=rcnt.at[d - 1], send_sem=s_cnt.at[d - 1],
            recv_sem=r_cnt.at[d - 1], device_id={"tm": q}, device_id_type=MESH)

    pl.semaphore_wait(barrier, tm - 1 + space - 1)
    every(tm, lambda d: cnt_copy(d).start(), 1)

    def sort(c):
        for k in range(chunks):
            rows_in(c, k).wait()
            for n in range(tm):
                sl = slice(n * w, (n + 1) * w)
                y = jnp.dot(perm[k], X[c, k * CHUNK:(k + 1) * CHUNK, sl], preferred_element_type=F32)
                Xs[c, k * tiles:(k + 1) * tiles, :, sl] = y[:CHUNK].astype(BF16).reshape(tiles, TILE, w)
                some = y[CHUNK:]
                if k > 0:
                    some = some + sums[n]
                if k < chunks - 1:
                    sums[n] = some
                else:
                    for q in range(tm):
                        ssend[q, c, n * own_rows:(n + 1) * own_rows, :] = some[q * own_rows:(q + 1) * own_rows]
        every(tm, lambda d: sum_copy(c, d).start(), 1)

    every(comp, sort)
    scopy.wait()

    def mj_copy(d, q):
        at = pl.ds(pl.multiple_of(q * 8, 8), 8)
        return pltpu.make_async_remote_copy(
            src_ref=mj.at[at], dst_ref=mj.at[at], send_sem=s_mj.at[d - 1], recv_sem=r_mj.at[d - 1],
            device_id={"tm": lax.rem(me_t + d, tm)}, device_id_type=MESH)

    ocopy = pltpu.make_async_copy(meanv, mean_out, osem)

    def means():
        every(tm, lambda d: cnt_copy(d).wait(), 1)
        every(comp * (tm - 1), lambda i: sum_copy(i // (tm - 1), i % (tm - 1) + 1).wait())
        total_cnt = cnt[me_t]
        for d in range(tm - 1):
            total_cnt = total_cnt + rcnt[d]
        for c in range(comp):
            tot = ssend[me_t, c]
            for d in range(tm - 1):
                tot = tot + rsum[d, c]
            m = tot / total_cnt[:, 0:1]
            mean[c] = m.astype(BF16)
            for n in range(tm):
                meanv[c, :, n * w:(n + 1) * w] = m[n * own_rows:(n + 1) * own_rows].astype(BF16)
        ocopy.start()
        at = [metas[OWNER, me_t * own_rows + i] for i in range(own_rows)]
        tall = (own_rows * nm, bins)

        def some(n, picked):
            p = jnp.zeros(tall, F32)
            sl = pl.ds(pl.multiple_of(n * w, w), w)
            for c in range(comp):
                lhs = jnp.concatenate([mo[c, a, :, sl] for a in at], 0)
                p += lax.dot_general(lhs, mean[c], NT, preferred_element_type=F32)
            return picked + jnp.where(iota(tall, 1) == n * own_rows + iota(tall, 0) // nm, p, 0.0)

        picked = lax.fori_loop(0, tm, some, jnp.zeros(tall, F32))
        flat = picked[:nm]
        for i in range(1, own_rows):
            flat = flat + picked[i * nm:(i + 1) * nm]
        flat = flat.T
        mine = flat[:own_rows]
        for n in range(1, tm):
            mine = mine + flat[n * own_rows:(n + 1) * own_rows]
        mj[pl.ds(pl.multiple_of(me_t * 8, 8), 8)] = jnp.concatenate(
            [mine, jnp.zeros((8 - own_rows, nm), F32)], 0)
        every(tm, lambda d: mj_copy(d, me_t).start(), 1)

    split = pairs - 3

    def project(p):
        @pl.when(p < split)
        def _():
            fetch(2 * p).wait()
            fetch(2 * p + 1).wait()

        @pl.when(p == split)
        def _():
            every(bins, lambda b: fetch(b).wait(), 2 * split)
            means()

        prod = jnp.zeros((slots, 2 * nm), F32)
        for c in range(comp):
            sorted_rows = jnp.concatenate([Xs[c, metas[TABLE, p * 128 + s]] for s in range(slots // TILE)], 0)
            prod += lax.dot_general(
                sorted_rows, mo[c, pl.ds(2 * p, 2)].reshape(2 * nm, cells), NT, preferred_element_type=F32)
        for b in range(2):
            prods[pl.ds(pl.multiple_of((2 * p + b) * slots, TILE), slots)] = prod[:, b * nm:(b + 1) * nm]

    every(pairs, project)

    def mj_done(d):
        mj_copy(d, me_t).wait_send()
        mj_copy(d, lax.rem(me_t + tm - d, tm)).wait_recv()

    every(tm, mj_done, 1)
    rest = mj[...]
    total = jnp.zeros((rows, nm), F32)
    for _ in range(3):
        term = rest.astype(BF16)
        rest = rest - term.astype(F32)
        total = total + jnp.dot(byrow[:, :mj_rows], term, preferred_element_type=F32)
    fix[...] = total

    def part_rows(s, h):
        return pl.ds(pl.multiple_of(s * blk + h * part, TILE), part)

    def rs_copy(h, d):
        return pltpu.make_async_remote_copy(
            src_ref=sendc.at[h, d], dst_ref=rsc.at[h, d - 1], send_sem=s_rs.at[h, d - 1],
            recv_sem=r_rs.at[h, d - 1], device_id={"space": lax.rem(me_s + d, space)}, device_id_type=MESH)

    def unsort(i):
        h, d = i // space, lax.rem(i + 1, space)
        q = lax.rem(me_s + d, space)

        def some(g, _):
            for r in range(UNROLL):
                t = q * blk + h * part + g * UNROLL + r
                acc[h, pl.ds(g * UNROLL + r, 1)] = prods[pl.ds(metas[KEY, t], 1)]
            return 0

        lax.fori_loop(0, part // UNROLL, some, 0)
        v = acc[h] - fix[part_rows(q, h)]
        acc[h] = v
        sendc[h, d] = v.astype(BF16)

        @pl.when(d > 0)
        def _():
            rs_copy(h, d).start()

    every(HALVES * space, unsort)

    def ag_copy(h, d, s):
        return pltpu.make_async_remote_copy(
            src_ref=agc.at[h], dst_ref=coef_out.at[part_rows(s, h)], send_sem=s_ag.at[h, d - 1],
            recv_sem=r_ag.at[h, d - 1], device_id={"space": lax.rem(me_s + d, space)}, device_id_type=MESH)

    def keep(h):
        return pltpu.make_async_copy(agc.at[h], coef_out.at[part_rows(me_s, h)], osem_c.at[h])

    def gather(h):
        def add(d, tot):
            rs_copy(h, d).wait()
            return tot + rsc[h, d - 1].astype(F32)

        agc[h] = lax.fori_loop(1, space, add, acc[h]).astype(BF16)
        every(space, lambda d: ag_copy(h, d, me_s).start(), 1)
        keep(h).start()

    every(HALVES, gather)
    ocopy.wait()

    def done(i):
        h, d = i // (space - 1), i % (space - 1) + 1
        ag_copy(h, d, me_s).wait_send()
        ag_copy(h, d, lax.rem(me_s + space - d, space)).wait_recv()

    every(HALVES * (space - 1), done)
    every(HALVES, lambda h: keep(h).wait())


def finish(coef, mean, coef_out, mean_out):
    coef_out[...] = coef[...].astype(F32)
    mean_out[...] = mean[...]


def on_device(snaps, phase_bin, owner_order, modes):
    rows, comp, cells = snaps.shape
    bins, nm = modes.shape[0], modes.shape[1]
    tm, space = lax.axis_size("tm"), lax.axis_size("space")
    blk, w, own_rows = rows // space, cells // tm, bins // tm
    chunks, slots = rows // CHUNK, slots_of(rows)
    ownrow = owner_order.reshape(1, bins)
    vm = pl.BlockSpec(memory_space=pltpu.VMEM)
    hbm = pl.BlockSpec(memory_space=pl.ANY)
    dma = pltpu.SemaphoreType.DMA
    binrow = phase_bin.reshape(1, rows)
    meta = pl.pallas_call(
        functools.partial(plan, tm),
        out_shape=jax.ShapeDtypeStruct((8, rows), I32),
        in_specs=[vm, vm],
        out_specs=vm,
    )(binrow, ownrow)
    coef, mean = pl.pallas_call(
        functools.partial(kernel, tm, space),
        out_shape=(
            jax.ShapeDtypeStruct((rows, nm), BF16),
            jax.ShapeDtypeStruct((comp, own_rows, cells), BF16),
        ),
        in_specs=[hbm, hbm, hbm],
        out_specs=(hbm, hbm),
        scratch_shapes=[
            pltpu.VMEM((8, rows), I32),
            pltpu.SMEM((8, rows), I32),
            pltpu.VMEM((comp, own_rows, cells), BF16),
            pltpu.VMEM((comp, rows, cells), BF16),
            pltpu.VMEM((comp, rows // TILE, TILE, cells), BF16),
            pltpu.VMEM((comp, bins, nm, cells), BF16),
            pltpu.VMEM((chunks, CHUNK + bins, CHUNK), BF16),
            pltpu.VMEM((bins * slots, nm), F32),
            pltpu.VMEM((tm, bins, w), F32),
            pltpu.VMEM((tm, comp, bins, w), F32),
            pltpu.VMEM((tm - 1, comp, bins, w), F32),
            pltpu.VMEM((tm, bins, 128), F32),
            pltpu.VMEM((tm - 1, bins, 128), F32),
            pltpu.VMEM((comp, bins, w), BF16),
            pltpu.VMEM((tm * 8, nm), F32),
            pltpu.VMEM((rows, 128), BF16),
            pltpu.VMEM((rows, nm), F32),
            pltpu.VMEM((HALVES, blk // HALVES, nm), F32),
            pltpu.VMEM((HALVES, space, blk // HALVES, nm), BF16),
            pltpu.VMEM((HALVES, space - 1, blk // HALVES, nm), BF16),
            pltpu.VMEM((HALVES, blk // HALVES, nm), BF16),
            dma(()), dma(()), dma(()), dma((HALVES,)), dma((comp, chunks)), dma((bins,)),
            dma((tm - 1, comp)), dma((tm - 1, comp)), dma((tm - 1,)), dma((tm - 1,)), dma((tm - 1,)), dma((tm - 1,)),
            dma((HALVES, space - 1)), dma((HALVES, space - 1)), dma((HALVES, space - 1)), dma((HALVES, space - 1)),
        ],
        compiler_params=pltpu.CompilerParams(
            collective_id=0, has_side_effects=True, vmem_limit_bytes=61 * 1024 * 1024
        ),
        cost_estimate=pl.CostEstimate(
            flops=2 * slots * bins * nm * comp * cells,
            bytes_accessed=2 * comp * cells * (rows + bins * nm), transcendentals=0),
    )(meta, snaps.transpose(1, 0, 2), modes.transpose(0, 2, 1, 3))
    coef, mean = pl.pallas_call(
        finish,
        out_shape=(
            jax.ShapeDtypeStruct((rows, nm), F32),
            jax.ShapeDtypeStruct((comp, own_rows, cells), BF16),
        ),
        in_specs=[vm, vm],
        out_specs=(vm, vm),
    )(coef, mean)
    return mean.transpose(1, 0, 2), coef


def solution(mesh):
    in_specs = (P("tm", None, "space"), P("tm"), P(), P(None, None, None, "space"))
    out_specs = (P("tm", None, "space"), P("tm", None))
    return jax.shard_map(
        on_device, mesh=mesh, in_specs=in_specs, out_specs=out_specs, check_vma=False
    )
```

```python
import functools

import jax
import jax.numpy as jnp
from jax import lax
from jax.experimental import pallas as pl
from jax.experimental.pallas import tpu as pltpu
from jax.sharding import PartitionSpec as P

MESH = pl.DeviceIdType.MESH
F32 = jnp.float32
BF16 = jnp.bfloat16
I32 = jnp.int32
NT = (((1,), (1,)), ((), ()))
CHUNK = 256
TILE = 16
UNROLL = 32
HALVES = 2
CAP = 128


def slots_of(rows):
    chunks = rows // CHUNK
    return TILE * ((2 * CAP + (TILE - 2) * chunks) // TILE + chunks)


def iota(shape, dim):
    return lax.broadcasted_iota(I32, shape, dim)


def ones_where(cond):
    return jnp.where(cond, 1.0, 0.0)


def owners(ownrow, rank_of_row):
    bins = ownrow.shape[1]
    return jnp.sum(jnp.where(rank_of_row == iota((bins, bins), 1), ownrow, 0), axis=1, keepdims=True)


def sums_before(x, dim, length):
    total, at, step = x, iota(x.shape, dim) % length, 1
    while step < length:
        total = total + jnp.where(at >= step, pltpu.roll(total, step, dim), 0)
        step *= 2
    return total - x


def kernel(
    tm, space, bins_in, owners_in, snaps, modes, coef_out, mean_out,
    binv, ownv, owns, tablev, tables, keyv, keys, meanv, X, Xs, mo, perm, prods, sums, ssend, rsum, cnt, rcnt, mean, mj,
    byrow, fix, acc, sendc, rsc, agc,
    vsem, osem, osem_c, xsem, msem, s_sum, r_sum, s_cnt, r_cnt, s_mj, r_mj, s_rs, r_rs, s_ag, r_ag,
):
    comp, rows, cells = snaps.shape
    bins, nm = modes.shape[0], modes.shape[2]
    pairs, chunks, tiles = bins // 2, rows // CHUNK, CHUNK // TILE
    slots = slots_of(rows)
    own_rows = bins // tm
    w = cells // tm
    blk = rows // space
    part = blk // HALVES
    mj_rows = 8 * tm
    me_t = lax.axis_index("tm")
    me_s = lax.axis_index("space")

    def every(n, f, first=0):
        lax.fori_loop(first, n, lambda i, _: (f(i), 0)[1], 0)

    first_copies = [
        pltpu.make_async_copy(bins_in, binv, vsem.at[0]), pltpu.make_async_copy(owners_in, ownv, vsem.at[1]),
        pltpu.make_async_copy(owners_in, owns, vsem.at[2])]
    for cp in first_copies:
        cp.start()

    def rows_in(c, k):
        sl = pl.ds(pl.multiple_of(k * CHUNK, CHUNK), CHUNK)
        return pltpu.make_async_copy(snaps.at[c, sl], X.at[c, sl], xsem.at[c, k])

    every(comp * chunks, lambda i: rows_in(i // chunks, i % chunks).start())

    def fetch(b):
        return pltpu.make_async_copy(modes.at[b], mo.at[:, b], msem.at[b])

    every(bins, lambda b: fetch(b).start())

    barrier = pltpu.get_barrier_semaphore()
    for d in range(1, tm):
        pl.semaphore_signal(barrier, inc=1, device_id={"tm": lax.rem(me_t + d, tm)}, device_id_type=MESH)
    for d in range(1, space):
        pl.semaphore_signal(barrier, inc=1, device_id={"space": lax.rem(me_s + d, space)}, device_id_type=MESH)

    for cp in first_copies:
        cp.wait()
    binrow = binv[...]
    ownrow = ownv[...]

    groups = chunks * bins
    hot = jnp.concatenate(
        [jnp.where(binrow[:, k * CHUNK:(k + 1) * CHUNK] == iota((bins, CHUNK), 0), 1, 0) for k in range(chunks)], 0)
    rank = sums_before(hot, 1, CHUNK)
    count = jnp.broadcast_to(jnp.sum(hot, axis=1, keepdims=True), (groups, 128))
    base = sums_before(count, 0, bins)
    even = iota((groups, 128), 0) % 2 == 0
    pair_base = jnp.where(even, base, pltpu.roll(base, 1, 0))
    pair_count = count + jnp.where(even, pltpu.roll(count, groups - 1, 0), pltpu.roll(count, 1, 0))
    first = pair_base // TILE
    n_tiles = jnp.where(pair_count > 0, (pair_base + pair_count - 1) // TILE - first + 1, 0)
    place = iota((bins, 128), 1)
    skip = jnp.zeros((bins, 128), I32)
    table = jnp.zeros((bins, 128), I32)
    own = owners(ownrow, iota((bins, bins), 0))
    j = iota((bins, CHUNK), 0)
    mj_row = 8 * (j // own_rows) + j % own_rows
    for k in range(chunks):
        sl, here = slice(k * CHUNK, (k + 1) * CHUNK), slice(k * bins, (k + 1) * bins)
        bk, f, nk = binrow[:, sl], first[here], n_tiles[here]
        table = table + jnp.where((place >= skip) & (place < skip + nk), tiles * k + f + place - skip, 0)
        slot = jnp.sum(hot[here] * (base[here][:, 0:1] + rank[here]), axis=0, keepdims=True)
        shift = jnp.sum(hot[here] * (TILE * (skip - f))[:, 0:1], axis=0, keepdims=True)
        keyv[:, sl] = slot + shift + bk * slots
        perm[k, :CHUNK, :] = ones_where(slot == iota((CHUNK, CHUNK), 0)).astype(BF16)
        by_owner = bk == own
        perm[k, CHUNK:, :] = ones_where(by_owner).astype(BF16)
        mean_row = jnp.sum(jnp.where(by_owner, mj_row, 0), axis=0, keepdims=True)
        for g in range(CHUNK // 128):
            at_row = jnp.broadcast_to(mean_row[:, g * 128:(g + 1) * 128], (128, 128)).T
            byrow[k * CHUNK + g * 128:k * CHUNK + (g + 1) * 128, :] = ones_where(
                iota((128, 128), 1) == at_row).astype(BF16)
        skip = skip + nk
    tablev[...] = table
    plan_copies = [pltpu.make_async_copy(tablev, tables, vsem.at[3]), pltpu.make_async_copy(keyv, keys, vsem.at[4])]
    for cp in plan_copies:
        cp.start()
    for q in range(tm):
        mine = owners(ownrow, q * own_rows + iota((bins, bins), 0) % own_rows)
        cnt[q] = jnp.broadcast_to(
            jnp.sum(ones_where(mine == binrow), axis=1, keepdims=True), (bins, 128))
    def sum_copy(c, d):
        q = lax.rem(me_t + d, tm)
        return pltpu.make_async_remote_copy(
            src_ref=ssend.at[q, c], dst_ref=rsum.at[d - 1, c], send_sem=s_sum.at[d - 1, c],
            recv_sem=r_sum.at[d - 1, c], device_id={"tm": q}, device_id_type=MESH)

    def cnt_copy(d):
        q = lax.rem(me_t + d, tm)
        return pltpu.make_async_remote_copy(
            src_ref=cnt.at[q], dst_ref=rcnt.at[d - 1], send_sem=s_cnt.at[d - 1],
            recv_sem=r_cnt.at[d - 1], device_id={"tm": q}, device_id_type=MESH)

    def sort(c):
        for k in range(chunks):
            rows_in(c, k).wait()
            for n in range(tm):
                sl = slice(n * w, (n + 1) * w)
                y = jnp.dot(perm[k], X[c, k * CHUNK:(k + 1) * CHUNK, sl], preferred_element_type=F32)
                Xs[c, k * tiles:(k + 1) * tiles, :, sl] = y[:CHUNK].astype(BF16).reshape(tiles, TILE, w)
                some = y[CHUNK:]
                if k > 0:
                    some = some + sums[n]
                if k < chunks - 1:
                    sums[n] = some
                else:
                    for q in range(tm):
                        ssend[q, c, n * own_rows:(n + 1) * own_rows, :] = some[q * own_rows:(q + 1) * own_rows]

        @pl.when(c == 0)
        def _():
            pl.semaphore_wait(barrier, tm - 1 + space - 1)
            every(tm, lambda d: cnt_copy(d).start(), 1)

        every(tm, lambda d: sum_copy(c, d).start(), 1)

    every(comp, sort)
    for cp in plan_copies:
        cp.wait()

    def mj_copy(d, q):
        at = pl.ds(pl.multiple_of(q * 8, 8), 8)
        return pltpu.make_async_remote_copy(
            src_ref=mj.at[at], dst_ref=mj.at[at], send_sem=s_mj.at[d - 1], recv_sem=r_mj.at[d - 1],
            device_id={"tm": lax.rem(me_t + d, tm)}, device_id_type=MESH)

    ocopy = pltpu.make_async_copy(meanv, mean_out, osem)

    def means():
        every(tm, lambda d: cnt_copy(d).wait(), 1)
        every(comp * (tm - 1), lambda i: sum_copy(i // (tm - 1), i % (tm - 1) + 1).wait())
        total_cnt = cnt[me_t]
        for d in range(tm - 1):
            total_cnt = total_cnt + rcnt[d]
        for c in range(comp):
            tot = ssend[me_t, c]
            for d in range(tm - 1):
                tot = tot + rsum[d, c]
            m = tot / total_cnt[:, 0:1]
            mean[c] = m.astype(BF16)
            for n in range(tm):
                meanv[c, :, n * w:(n + 1) * w] = m[n * own_rows:(n + 1) * own_rows].astype(BF16)
        ocopy.start()
        at = [owns[0, me_t * own_rows + i] for i in range(own_rows)]
        tall = (own_rows * nm, bins)

        def some(n, picked):
            p = jnp.zeros(tall, F32)
            sl = pl.ds(pl.multiple_of(n * w, w), w)
            for c in range(comp):
                lhs = jnp.concatenate([mo[c, a, :, sl] for a in at], 0)
                p += lax.dot_general(lhs, mean[c], NT, preferred_element_type=F32)
            return picked + jnp.where(iota(tall, 1) == n * own_rows + iota(tall, 0) // nm, p, 0.0)

        picked = lax.fori_loop(0, tm, some, jnp.zeros(tall, F32))
        flat = picked[:nm]
        for i in range(1, own_rows):
            flat = flat + picked[i * nm:(i + 1) * nm]
        flat = flat.T
        mine = flat[:own_rows]
        for n in range(1, tm):
            mine = mine + flat[n * own_rows:(n + 1) * own_rows]
        mj[pl.ds(pl.multiple_of(me_t * 8, 8), 8)] = jnp.concatenate(
            [mine, jnp.zeros((8 - own_rows, nm), F32)], 0)
        every(tm, lambda d: mj_copy(d, me_t).start(), 1)

    split = pairs - 3

    def project(p):
        @pl.when(p < split)
        def _():
            fetch(2 * p).wait()
            fetch(2 * p + 1).wait()

        @pl.when(p == split)
        def _():
            every(bins, lambda b: fetch(b).wait(), 2 * split)
            means()

        prod = jnp.zeros((slots, 2 * nm), F32)
        for c in range(comp):
            sorted_rows = jnp.concatenate([Xs[c, tables[2 * p, s]] for s in range(slots // TILE)], 0)
            prod += lax.dot_general(
                sorted_rows, mo[c, pl.ds(2 * p, 2)].reshape(2 * nm, cells), NT, preferred_element_type=F32)
        for b in range(2):
            prods[pl.ds(pl.multiple_of((2 * p + b) * slots, TILE), slots)] = prod[:, b * nm:(b + 1) * nm]

    every(pairs, project)

    def mj_done(d):
        mj_copy(d, me_t).wait_send()
        mj_copy(d, lax.rem(me_t + tm - d, tm)).wait_recv()

    every(tm, mj_done, 1)
    rest = mj[...]
    total = jnp.zeros((rows, nm), F32)
    for _ in range(3):
        term = rest.astype(BF16)
        rest = rest - term.astype(F32)
        total = total + jnp.dot(byrow[:, :mj_rows], term, preferred_element_type=F32)
    fix[...] = total

    def part_rows(s, h):
        return pl.ds(pl.multiple_of(s * blk + h * part, TILE), part)

    def rs_copy(h, d):
        return pltpu.make_async_remote_copy(
            src_ref=sendc.at[h, d], dst_ref=rsc.at[h, d - 1], send_sem=s_rs.at[h, d - 1],
            recv_sem=r_rs.at[h, d - 1], device_id={"space": lax.rem(me_s + d, space)}, device_id_type=MESH)

    def unsort(i):
        h, d = i // space, lax.rem(i + 1, space)
        q = lax.rem(me_s + d, space)

        def some(g, _):
            for r in range(UNROLL):
                t = q * blk + h * part + g * UNROLL + r
                acc[h, pl.ds(g * UNROLL + r, 1)] = prods[pl.ds(keys[0, t], 1)]
            return 0

        lax.fori_loop(0, part // UNROLL, some, 0)
        v = acc[h] - fix[part_rows(q, h)]
        acc[h] = v
        sendc[h, d] = v.astype(BF16)

        @pl.when(d > 0)
        def _():
            rs_copy(h, d).start()

    every(HALVES * space, unsort)

    def ag_copy(h, d, s):
        return pltpu.make_async_remote_copy(
            src_ref=agc.at[h], dst_ref=coef_out.at[part_rows(s, h)], send_sem=s_ag.at[h, d - 1],
            recv_sem=r_ag.at[h, d - 1], device_id={"space": lax.rem(me_s + d, space)}, device_id_type=MESH)

    def keep(h):
        return pltpu.make_async_copy(agc.at[h], coef_out.at[part_rows(me_s, h)], osem_c.at[h])

    def gather(h):
        def add(d, tot):
            rs_copy(h, d).wait()
            return tot + rsc[h, d - 1].astype(F32)

        agc[h] = lax.fori_loop(1, space, add, acc[h]).astype(BF16)
        every(space, lambda d: ag_copy(h, d, me_s).start(), 1)
        keep(h).start()

    every(HALVES, gather)
    ocopy.wait()

    def done(i):
        h, d = i // (space - 1), i % (space - 1) + 1
        ag_copy(h, d, me_s).wait_send()
        ag_copy(h, d, lax.rem(me_s + space - d, space)).wait_recv()

    every(HALVES * (space - 1), done)
    every(HALVES, lambda h: keep(h).wait())


def finish(coef, mean, coef_out, mean_out):
    coef_out[...] = coef[...].astype(F32)
    mean_out[...] = mean[...]


def on_device(snaps, phase_bin, owner_order, modes):
    rows, comp, cells = snaps.shape
    bins, nm = modes.shape[0], modes.shape[1]
    tm, space = lax.axis_size("tm"), lax.axis_size("space")
    blk, w, own_rows = rows // space, cells // tm, bins // tm
    chunks, slots = rows // CHUNK, slots_of(rows)
    ownrow = owner_order.reshape(1, bins)
    vm = pl.BlockSpec(memory_space=pltpu.VMEM)
    hbm = pl.BlockSpec(memory_space=pl.ANY)
    dma = pltpu.SemaphoreType.DMA
    binrow = phase_bin.reshape(1, rows)
    coef, mean = pl.pallas_call(
        functools.partial(kernel, tm, space),
        out_shape=(
            jax.ShapeDtypeStruct((rows, nm), BF16),
            jax.ShapeDtypeStruct((comp, own_rows, cells), BF16),
        ),
        in_specs=[hbm, hbm, hbm, hbm],
        out_specs=(hbm, hbm),
        scratch_shapes=[
            pltpu.VMEM((1, rows), I32),
            pltpu.VMEM((1, bins), I32),
            pltpu.SMEM((1, bins), I32),
            pltpu.VMEM((bins, 128), I32),
            pltpu.SMEM((bins, 128), I32),
            pltpu.VMEM((1, rows), I32),
            pltpu.SMEM((1, rows), I32),
            pltpu.VMEM((comp, own_rows, cells), BF16),
            pltpu.VMEM((comp, rows, cells), BF16),
            pltpu.VMEM((comp, rows // TILE, TILE, cells), BF16),
            pltpu.VMEM((comp, bins, nm, cells), BF16),
            pltpu.VMEM((chunks, CHUNK + bins, CHUNK), BF16),
            pltpu.VMEM((bins * slots, nm), F32),
            pltpu.VMEM((tm, bins, w), F32),
            pltpu.VMEM((tm, comp, bins, w), F32),
            pltpu.VMEM((tm - 1, comp, bins, w), F32),
            pltpu.VMEM((tm, bins, 128), F32),
            pltpu.VMEM((tm - 1, bins, 128), F32),
            pltpu.VMEM((comp, bins, w), BF16),
            pltpu.VMEM((tm * 8, nm), F32),
            pltpu.VMEM((rows, 128), BF16),
            pltpu.VMEM((rows, nm), F32),
            pltpu.VMEM((HALVES, blk // HALVES, nm), F32),
            pltpu.VMEM((HALVES, space, blk // HALVES, nm), BF16),
            pltpu.VMEM((HALVES, space - 1, blk // HALVES, nm), BF16),
            pltpu.VMEM((HALVES, blk // HALVES, nm), BF16),
            dma((5,)), dma(()), dma((HALVES,)), dma((comp, chunks)), dma((bins,)),
            dma((tm - 1, comp)), dma((tm - 1, comp)), dma((tm - 1,)), dma((tm - 1,)), dma((tm - 1,)), dma((tm - 1,)),
            dma((HALVES, space - 1)), dma((HALVES, space - 1)), dma((HALVES, space - 1)), dma((HALVES, space - 1)),
        ],
        compiler_params=pltpu.CompilerParams(
            collective_id=0, has_side_effects=True, vmem_limit_bytes=61 * 1024 * 1024
        ),
        cost_estimate=pl.CostEstimate(
            flops=2 * slots * bins * nm * comp * cells,
            bytes_accessed=2 * comp * cells * (rows + bins * nm), transcendentals=0),
    )(binrow, ownrow, snaps.transpose(1, 0, 2), modes.transpose(0, 2, 1, 3))
    coef, mean = pl.pallas_call(
        finish,
        out_shape=(
            jax.ShapeDtypeStruct((rows, nm), F32),
            jax.ShapeDtypeStruct((comp, own_rows, cells), BF16),
        ),
        in_specs=[vm, vm],
        out_specs=(vm, vm),
    )(coef, mean)
    return mean.transpose(1, 0, 2), coef


def solution(mesh):
    in_specs = (P("tm", None, "space"), P("tm"), P(), P(None, None, None, "space"))
    out_specs = (P("tm", None, "space"), P("tm", None))
    return jax.shard_map(
        on_device, mesh=mesh, in_specs=in_specs, out_specs=out_specs, check_vma=False
    )
```

```python
import functools

import jax
import jax.numpy as jnp
from jax import lax
from jax.experimental import pallas as pl
from jax.experimental.pallas import tpu as pltpu
from jax.sharding import PartitionSpec as P

MESH = pl.DeviceIdType.MESH
F32 = jnp.float32
BF16 = jnp.bfloat16
I32 = jnp.int32
NT = (((1,), (1,)), ((), ()))
CHUNK = 256
TILE = 16
HALVES = 2
CAP = 128


def slots_of(rows):
    chunks = rows // CHUNK
    return TILE * ((2 * CAP + (TILE - 2) * chunks) // TILE + chunks)


def iota(shape, dim):
    return lax.broadcasted_iota(I32, shape, dim)


def ones_where(cond):
    return jnp.where(cond, 1.0, 0.0)


def owners(ownrow, rank_of_row):
    bins = ownrow.shape[1]
    return jnp.sum(jnp.where(rank_of_row == iota((bins, bins), 1), ownrow, 0), axis=1, keepdims=True)


def sums_before(x, dim, length):
    total, at, step = x, iota(x.shape, dim) % length, 1
    while step < length:
        total = total + jnp.where(at >= step, pltpu.roll(total, step, dim), 0)
        step *= 2
    return total - x


def kernel(
    tm, space, bins_in, owners_in, snaps, modes, coef_out, mean_out,
    binv, ownv, owns, tablev, tables, keyv, keys, meanv, X, Xs, mo, perm, prods, sums, ssend, rsum, cnt, rcnt, mean, mj,
    byrow, terms, acc, sendc, rsc, agc,
    vsem, osem, osem_c, xsem, msem, s_sum, r_sum, s_cnt, r_cnt, s_mj, r_mj, s_rs, r_rs, s_ag, r_ag,
):
    comp, rows, cells = snaps.shape
    bins, nm = modes.shape[0], modes.shape[2]
    pairs, chunks, tiles = bins // 2, rows // CHUNK, CHUNK // TILE
    slots = slots_of(rows)
    own_rows = bins // tm
    w = cells // tm
    blk = rows // space
    part = blk // HALVES
    mj_rows = 8 * tm
    me_t = lax.axis_index("tm")
    me_s = lax.axis_index("space")

    def every(n, f, first=0):
        lax.fori_loop(first, n, lambda i, _: (f(i), 0)[1], 0)

    first_copies = [
        pltpu.make_async_copy(bins_in, binv, vsem.at[0]), pltpu.make_async_copy(owners_in, ownv, vsem.at[1]),
        pltpu.make_async_copy(owners_in, owns, vsem.at[2])]
    for cp in first_copies:
        cp.start()

    def rows_in(c, k):
        sl = pl.ds(pl.multiple_of(k * CHUNK, CHUNK), CHUNK)
        return pltpu.make_async_copy(snaps.at[c, sl], X.at[c, sl], xsem.at[c, k])

    every(comp * chunks, lambda i: rows_in(i // chunks, i % chunks).start())

    def fetch(b):
        return pltpu.make_async_copy(modes.at[b], mo.at[:, b], msem.at[b])

    every(bins, lambda b: fetch(b).start())

    barrier = pltpu.get_barrier_semaphore()
    for d in range(1, tm):
        pl.semaphore_signal(barrier, inc=1, device_id={"tm": lax.rem(me_t + d, tm)}, device_id_type=MESH)
    for d in range(1, space):
        pl.semaphore_signal(barrier, inc=1, device_id={"space": lax.rem(me_s + d, space)}, device_id_type=MESH)

    for cp in first_copies:
        cp.wait()
    binrow = binv[...]
    ownrow = ownv[...]

    groups = chunks * bins
    hot = jnp.concatenate(
        [jnp.where(binrow[:, k * CHUNK:(k + 1) * CHUNK] == iota((bins, CHUNK), 0), 1, 0) for k in range(chunks)], 0)
    rank = sums_before(hot, 1, CHUNK)
    count = jnp.broadcast_to(jnp.sum(hot, axis=1, keepdims=True), (groups, 128))
    base = sums_before(count, 0, bins)
    even = iota((groups, 128), 0) % 2 == 0
    pair_base = jnp.where(even, base, pltpu.roll(base, 1, 0))
    pair_count = count + jnp.where(even, pltpu.roll(count, groups - 1, 0), pltpu.roll(count, 1, 0))
    first = pair_base // TILE
    n_tiles = jnp.where(pair_count > 0, (pair_base + pair_count - 1) // TILE - first + 1, 0)
    place = iota((bins, 128), 1)
    skip = jnp.zeros((bins, 128), I32)
    table = jnp.zeros((bins, 128), I32)
    own = owners(ownrow, iota((bins, bins), 0))
    j = iota((bins, CHUNK), 0)
    mj_row = 8 * (j // own_rows) + j % own_rows
    for k in range(chunks):
        sl, here = slice(k * CHUNK, (k + 1) * CHUNK), slice(k * bins, (k + 1) * bins)
        bk, f, nk = binrow[:, sl], first[here], n_tiles[here]
        table = table + jnp.where((place >= skip) & (place < skip + nk), tiles * k + f + place - skip, 0)
        slot = jnp.sum(hot[here] * (base[here][:, 0:1] + rank[here]), axis=0, keepdims=True)
        shift = jnp.sum(hot[here] * (TILE * (skip - f))[:, 0:1], axis=0, keepdims=True)
        keyv[:, sl] = slot + shift + bk * slots
        perm[k, :CHUNK, :] = ones_where(slot == iota((CHUNK, CHUNK), 0)).astype(BF16)
        by_owner = bk == own
        perm[k, CHUNK:, :] = ones_where(by_owner).astype(BF16)
        mean_row = jnp.sum(jnp.where(by_owner, mj_row, 0), axis=0, keepdims=True)
        for g in range(CHUNK // 128):
            at_row = jnp.broadcast_to(mean_row[:, g * 128:(g + 1) * 128], (128, 128)).T
            byrow[k * CHUNK + g * 128:k * CHUNK + (g + 1) * 128, :] = ones_where(
                iota((128, 128), 1) == at_row).astype(BF16)
        skip = skip + nk
    tablev[...] = table
    plan_copies = [pltpu.make_async_copy(tablev, tables, vsem.at[3]), pltpu.make_async_copy(keyv, keys, vsem.at[4])]
    for cp in plan_copies:
        cp.start()
    for q in range(tm):
        mine = owners(ownrow, q * own_rows + iota((bins, bins), 0) % own_rows)
        cnt[q] = jnp.broadcast_to(
            jnp.sum(ones_where(mine == binrow), axis=1, keepdims=True), (bins, 128))
    def sum_copy(c, d):
        q = lax.rem(me_t + d, tm)
        return pltpu.make_async_remote_copy(
            src_ref=ssend.at[q, c], dst_ref=rsum.at[d - 1, c], send_sem=s_sum.at[d - 1, c],
            recv_sem=r_sum.at[d - 1, c], device_id={"tm": q}, device_id_type=MESH)

    def cnt_copy(d):
        q = lax.rem(me_t + d, tm)
        return pltpu.make_async_remote_copy(
            src_ref=cnt.at[q], dst_ref=rcnt.at[d - 1], send_sem=s_cnt.at[d - 1],
            recv_sem=r_cnt.at[d - 1], device_id={"tm": q}, device_id_type=MESH)

    def sort(c):
        for k in range(chunks):
            rows_in(c, k).wait()
            for n in range(tm):
                sl = slice(n * w, (n + 1) * w)
                y = jnp.dot(perm[k], X[c, k * CHUNK:(k + 1) * CHUNK, sl], preferred_element_type=F32)
                Xs[c, k * tiles:(k + 1) * tiles, :, sl] = y[:CHUNK].astype(BF16).reshape(tiles, TILE, w)
                some = y[CHUNK:]
                if k > 0:
                    some = some + sums[n]
                if k < chunks - 1:
                    sums[n] = some
                else:
                    for q in range(tm):
                        ssend[q, c, n * own_rows:(n + 1) * own_rows, :] = some[q * own_rows:(q + 1) * own_rows]

        @pl.when(c == 0)
        def _():
            pl.semaphore_wait(barrier, tm - 1 + space - 1)
            every(tm, lambda d: cnt_copy(d).start(), 1)

        every(tm, lambda d: sum_copy(c, d).start(), 1)

    every(comp, sort)
    for cp in plan_copies:
        cp.wait()

    def mj_copy(d, q):
        at = pl.ds(pl.multiple_of(q * 8, 8), 8)
        return pltpu.make_async_remote_copy(
            src_ref=mj.at[at], dst_ref=mj.at[at], send_sem=s_mj.at[d - 1], recv_sem=r_mj.at[d - 1],
            device_id={"tm": lax.rem(me_t + d, tm)}, device_id_type=MESH)

    ocopy = pltpu.make_async_copy(meanv, mean_out, osem)

    def means():
        every(tm, lambda d: cnt_copy(d).wait(), 1)
        every(comp * (tm - 1), lambda i: sum_copy(i // (tm - 1), i % (tm - 1) + 1).wait())
        total_cnt = cnt[me_t]
        for d in range(tm - 1):
            total_cnt = total_cnt + rcnt[d]
        for c in range(comp):
            tot = ssend[me_t, c]
            for d in range(tm - 1):
                tot = tot + rsum[d, c]
            m = tot / total_cnt[:, 0:1]
            for n in range(tm):
                mine = m[n * own_rows:(n + 1) * own_rows]
                meanv[c, :, n * w:(n + 1) * w] = mine.astype(BF16)
                mean[c, :, n * w:(n + 1) * w] = jnp.concatenate(
                    [mine, jnp.zeros((bins - own_rows, w), F32)], 0).astype(BF16)
        ocopy.start()
        at = [owns[0, me_t * own_rows + i] for i in range(own_rows)]
        tall = (own_rows * nm, bins)

        p = jnp.zeros(tall, F32)
        for c in range(comp):
            p += lax.dot_general(
                jnp.concatenate([mo[c, a] for a in at], 0), mean[c], NT, preferred_element_type=F32)
        flat = jnp.zeros((nm, bins), F32)
        for i in range(own_rows):
            flat = flat + jnp.where(iota((nm, bins), 1) == i, p[i * nm:(i + 1) * nm], 0.0)
        mine = flat.T[:own_rows]
        mj[pl.ds(pl.multiple_of(me_t * 8, 8), 8)] = jnp.concatenate(
            [mine, jnp.zeros((8 - own_rows, nm), F32)], 0)
        every(tm, lambda d: mj_copy(d, me_t).start(), 1)

    split = pairs - 3

    def project(p):
        @pl.when(p < split)
        def _():
            fetch(2 * p).wait()
            fetch(2 * p + 1).wait()

        @pl.when(p == split)
        def _():
            every(bins, lambda b: fetch(b).wait(), 2 * split)
            means()

        prod = jnp.zeros((slots, 2 * nm), F32)
        for c in range(comp):
            sorted_rows = jnp.concatenate([Xs[c, tables[2 * p, s]] for s in range(slots // TILE)], 0)
            prod += lax.dot_general(
                sorted_rows, mo[c, pl.ds(2 * p, 2)].reshape(2 * nm, cells), NT, preferred_element_type=F32)
        for b in range(2):
            prods[pl.ds(pl.multiple_of((2 * p + b) * slots, TILE), slots)] = prod[:, b * nm:(b + 1) * nm]

    every(pairs, project)

    def mj_done(d):
        mj_copy(d, me_t).wait_send()
        mj_copy(d, lax.rem(me_t + tm - d, tm)).wait_recv()

    every(tm, mj_done, 1)
    rest = mj[...]
    for i in range(3):
        term = rest.astype(BF16)
        rest = rest - term.astype(F32)
        terms[i] = term

    def part_rows(s, h):
        return pl.ds(pl.multiple_of(s * blk + h * part, TILE), part)

    def rs_copy(h, d):
        return pltpu.make_async_remote_copy(
            src_ref=sendc.at[h, d], dst_ref=rsc.at[h, d - 1], send_sem=s_rs.at[h, d - 1],
            recv_sem=r_rs.at[h, d - 1], device_id={"space": lax.rem(me_s + d, space)}, device_id_type=MESH)

    def unsort(i):
        h, d = i // space, lax.rem(i + 1, space)
        q = lax.rem(me_s + d, space)

        here = byrow[part_rows(q, h), :mj_rows]
        off = jnp.dot(here, terms[0], preferred_element_type=F32)
        for i in range(1, 3):
            off = off + jnp.dot(here, terms[i], preferred_element_type=F32)
        for r in range(part):
            acc[h, r:r + 1] = prods[pl.ds(keys[0, q * blk + h * part + r], 1)]
        v = acc[h] - off
        acc[h] = v
        sendc[h, d] = v.astype(BF16)

        @pl.when(d > 0)
        def _():
            rs_copy(h, d).start()

    every(HALVES * space, unsort)

    def ag_copy(h, d, s):
        return pltpu.make_async_remote_copy(
            src_ref=agc.at[h], dst_ref=coef_out.at[part_rows(s, h)], send_sem=s_ag.at[h, d - 1],
            recv_sem=r_ag.at[h, d - 1], device_id={"space": lax.rem(me_s + d, space)}, device_id_type=MESH)

    def keep(h):
        return pltpu.make_async_copy(agc.at[h], coef_out.at[part_rows(me_s, h)], osem_c.at[h])

    def gather(h):
        def add(d, tot):
            rs_copy(h, d).wait()
            return tot + rsc[h, d - 1].astype(F32)

        agc[h] = lax.fori_loop(1, space, add, acc[h]).astype(BF16)
        every(space, lambda d: ag_copy(h, d, me_s).start(), 1)
        keep(h).start()

    every(HALVES, gather)
    ocopy.wait()

    def done(i):
        h, d = i // (space - 1), i % (space - 1) + 1
        ag_copy(h, d, me_s).wait_send()
        ag_copy(h, d, lax.rem(me_s + space - d, space)).wait_recv()

    every(HALVES * (space - 1), done)
    every(HALVES, lambda h: keep(h).wait())


def finish(coef, mean, coef_out, mean_out):
    coef_out[...] = coef[...].astype(F32)
    mean_out[...] = mean[...]


def on_device(snaps, phase_bin, owner_order, modes):
    rows, comp, cells = snaps.shape
    bins, nm = modes.shape[0], modes.shape[1]
    tm, space = lax.axis_size("tm"), lax.axis_size("space")
    blk, w, own_rows = rows // space, cells // tm, bins // tm
    chunks, slots = rows // CHUNK, slots_of(rows)
    ownrow = owner_order.reshape(1, bins)
    vm = pl.BlockSpec(memory_space=pltpu.VMEM)
    hbm = pl.BlockSpec(memory_space=pl.ANY)
    dma = pltpu.SemaphoreType.DMA
    binrow = phase_bin.reshape(1, rows)
    coef, mean = pl.pallas_call(
        functools.partial(kernel, tm, space),
        out_shape=(
            jax.ShapeDtypeStruct((rows, nm), BF16),
            jax.ShapeDtypeStruct((comp, own_rows, cells), BF16),
        ),
        in_specs=[hbm, hbm, hbm, hbm],
        out_specs=(hbm, hbm),
        scratch_shapes=[
            pltpu.VMEM((1, rows), I32),
            pltpu.VMEM((1, bins), I32),
            pltpu.SMEM((1, bins), I32),
            pltpu.VMEM((bins, 128), I32),
            pltpu.SMEM((bins, 128), I32),
            pltpu.VMEM((1, rows), I32),
            pltpu.SMEM((1, rows), I32),
            pltpu.VMEM((comp, own_rows, cells), BF16),
            pltpu.VMEM((comp, rows, cells), BF16),
            pltpu.VMEM((comp, rows // TILE, TILE, cells), BF16),
            pltpu.VMEM((comp, bins, nm, cells), BF16),
            pltpu.VMEM((chunks, CHUNK + bins, CHUNK), BF16),
            pltpu.VMEM((bins * slots, nm), F32),
            pltpu.VMEM((tm, bins, w), F32),
            pltpu.VMEM((tm, comp, bins, w), F32),
            pltpu.VMEM((tm - 1, comp, bins, w), F32),
            pltpu.VMEM((tm, bins, 128), F32),
            pltpu.VMEM((tm - 1, bins, 128), F32),
            pltpu.VMEM((comp, bins, cells), BF16),
            pltpu.VMEM((tm * 8, nm), F32),
            pltpu.VMEM((rows, 128), BF16),
            pltpu.VMEM((3, 8 * tm, nm), BF16),
            pltpu.VMEM((HALVES, blk // HALVES, nm), F32),
            pltpu.VMEM((HALVES, space, blk // HALVES, nm), BF16),
            pltpu.VMEM((HALVES, space - 1, blk // HALVES, nm), BF16),
            pltpu.VMEM((HALVES, blk // HALVES, nm), BF16),
            dma((5,)), dma(()), dma((HALVES,)), dma((comp, chunks)), dma((bins,)),
            dma((tm - 1, comp)), dma((tm - 1, comp)), dma((tm - 1,)), dma((tm - 1,)), dma((tm - 1,)), dma((tm - 1,)),
            dma((HALVES, space - 1)), dma((HALVES, space - 1)), dma((HALVES, space - 1)), dma((HALVES, space - 1)),
        ],
        compiler_params=pltpu.CompilerParams(
            collective_id=0, has_side_effects=True, vmem_limit_bytes=61 * 1024 * 1024
        ),
        cost_estimate=pl.CostEstimate(
            flops=2 * slots * bins * nm * comp * cells,
            bytes_accessed=2 * comp * cells * (rows + bins * nm), transcendentals=0),
    )(binrow, ownrow, snaps.transpose(1, 0, 2), modes.transpose(0, 2, 1, 3))
    coef, mean = pl.pallas_call(
        finish,
        out_shape=(
            jax.ShapeDtypeStruct((rows, nm), F32),
            jax.ShapeDtypeStruct((comp, own_rows, cells), BF16),
        ),
        in_specs=[vm, vm],
        out_specs=(vm, vm),
    )(coef, mean)
    return mean.transpose(1, 0, 2), coef


def solution(mesh):
    in_specs = (P("tm", None, "space"), P("tm"), P(), P(None, None, None, "space"))
    out_specs = (P("tm", None, "space"), P("tm", None))
    return jax.shard_map(
        on_device, mesh=mesh, in_specs=in_specs, out_specs=out_specs, check_vma=False
    )
```

```python
import functools

import jax
import jax.numpy as jnp
from jax import lax
from jax.experimental import pallas as pl
from jax.experimental.pallas import tpu as pltpu
from jax.sharding import PartitionSpec as P

MESH = pl.DeviceIdType.MESH
F32 = jnp.float32
BF16 = jnp.bfloat16
I32 = jnp.int32
NT = (((1,), (1,)), ((), ()))
CHUNK = 256
TILE = 16
HALVES = 2
CAP = 128


def slots_of(rows):
    chunks = rows // CHUNK
    return TILE * ((2 * CAP + (TILE - 2) * chunks) // TILE + chunks)


def iota(shape, dim):
    return lax.broadcasted_iota(I32, shape, dim)


def ones_where(cond):
    return jnp.where(cond, 1.0, 0.0)


def owners(ownrow, rank_of_row):
    bins = ownrow.shape[1]
    return jnp.sum(jnp.where(rank_of_row == iota((bins, bins), 1), ownrow, 0), axis=1, keepdims=True)


def sums_before(x, dim, length):
    total, at, step = x, iota(x.shape, dim) % length, 1
    while step < length:
        total = total + jnp.where(at >= step, pltpu.roll(total, step, dim), 0)
        step *= 2
    return total - x


def kernel(
    tm, space, bins_in, owners_in, snaps, modes, coef_out, mean_out,
    binv, ownv, owns, tablev, tables, keyv, keys, meanv, X, Xs, mo, perm, prods, sums, ssend, rsum, cnt, rcnt, mean, mj,
    byrow, terms, acc, sendc, rsc, agc,
    vsem, osem, osem_c, xsem, msem, s_sum, r_sum, s_cnt, r_cnt, s_mj, r_mj, s_rs, r_rs, s_ag, r_ag,
):
    comp, rows, cells = snaps.shape
    bins, nm = modes.shape[0], modes.shape[2]
    pairs, chunks, tiles = bins // 2, rows // CHUNK, CHUNK // TILE
    slots = slots_of(rows)
    own_rows = bins // tm
    w = cells // tm
    blk = rows // space
    part = blk // HALVES
    mj_rows = 8 * tm
    me_t = lax.axis_index("tm")
    me_s = lax.axis_index("space")

    def every(n, f, first=0):
        lax.fori_loop(first, n, lambda i, _: (f(i), 0)[1], 0)

    first_copies = [
        pltpu.make_async_copy(bins_in, binv, vsem.at[0]), pltpu.make_async_copy(owners_in, ownv, vsem.at[1]),
        pltpu.make_async_copy(owners_in, owns, vsem.at[2])]
    for cp in first_copies:
        cp.start()

    def rows_in(c, k):
        sl = pl.ds(pl.multiple_of(k * CHUNK, CHUNK), CHUNK)
        return pltpu.make_async_copy(snaps.at[c, sl], X.at[c, sl], xsem.at[c, k])

    every(comp * chunks, lambda i: rows_in(i // chunks, i % chunks).start())

    def fetch(b):
        return pltpu.make_async_copy(modes.at[b], mo.at[:, b], msem.at[b])

    every(bins, lambda b: fetch(b).start())

    barrier = pltpu.get_barrier_semaphore()
    for d in range(1, tm):
        pl.semaphore_signal(barrier, inc=1, device_id={"tm": lax.rem(me_t + d, tm)}, device_id_type=MESH)
    for d in range(1, space):
        pl.semaphore_signal(barrier, inc=1, device_id={"space": lax.rem(me_s + d, space)}, device_id_type=MESH)

    for cp in first_copies:
        cp.wait()
    binrow = binv[...]
    ownrow = ownv[...]

    groups = chunks * bins
    hot = jnp.concatenate(
        [jnp.where(binrow[:, k * CHUNK:(k + 1) * CHUNK] == iota((bins, CHUNK), 0), 1, 0) for k in range(chunks)], 0)
    rank = sums_before(hot, 1, CHUNK)
    count = jnp.broadcast_to(jnp.sum(hot, axis=1, keepdims=True), (groups, 128))
    base = sums_before(count, 0, bins)
    even = iota((groups, 128), 0) % 2 == 0
    pair_base = jnp.where(even, base, pltpu.roll(base, 1, 0))
    pair_count = count + jnp.where(even, pltpu.roll(count, groups - 1, 0), pltpu.roll(count, 1, 0))
    first = pair_base // TILE
    n_tiles = jnp.where(pair_count > 0, (pair_base + pair_count - 1) // TILE - first + 1, 0)
    place = iota((bins, 128), 1)
    skip = jnp.zeros((bins, 128), I32)
    table = jnp.zeros((bins, 128), I32)
    own = owners(ownrow, iota((bins, bins), 0))
    j = iota((bins, CHUNK), 0)
    mj_row = 8 * (j // own_rows) + j % own_rows
    for k in range(chunks):
        sl, here = slice(k * CHUNK, (k + 1) * CHUNK), slice(k * bins, (k + 1) * bins)
        bk, f, nk = binrow[:, sl], first[here], n_tiles[here]
        table = table + jnp.where((place >= skip) & (place < skip + nk), tiles * k + f + place - skip, 0)
        slot = jnp.sum(hot[here] * (base[here][:, 0:1] + rank[here]), axis=0, keepdims=True)
        shift = jnp.sum(hot[here] * (TILE * (skip - f))[:, 0:1], axis=0, keepdims=True)
        keyv[:, sl] = slot + shift + bk * slots
        perm[k, :CHUNK, :] = ones_where(slot == iota((CHUNK, CHUNK), 0)).astype(BF16)
        by_owner = bk == own
        perm[k, CHUNK:, :] = ones_where(by_owner).astype(BF16)
        mean_row = jnp.sum(jnp.where(by_owner, mj_row, 0), axis=0, keepdims=True)
        for g in range(CHUNK // 128):
            at_row = jnp.broadcast_to(mean_row[:, g * 128:(g + 1) * 128], (128, 128)).T
            byrow[k * CHUNK + g * 128:k * CHUNK + (g + 1) * 128, :] = ones_where(
                iota((128, 128), 1) == at_row).astype(BF16)
        skip = skip + nk
    tablev[...] = table
    plan_copies = [pltpu.make_async_copy(tablev, tables, vsem.at[3]), pltpu.make_async_copy(keyv, keys, vsem.at[4])]
    for cp in plan_copies:
        cp.start()
    for q in range(tm):
        mine = owners(ownrow, q * own_rows + iota((bins, bins), 0) % own_rows)
        cnt[q] = jnp.broadcast_to(
            jnp.sum(ones_where(mine == binrow), axis=1, keepdims=True), (bins, 128))
    def sum_copy(c, d):
        q = lax.rem(me_t + d, tm)
        return pltpu.make_async_remote_copy(
            src_ref=ssend.at[q, c], dst_ref=rsum.at[d - 1, c], send_sem=s_sum.at[d - 1, c],
            recv_sem=r_sum.at[d - 1, c], device_id={"tm": q}, device_id_type=MESH)

    def cnt_copy(d):
        q = lax.rem(me_t + d, tm)
        return pltpu.make_async_remote_copy(
            src_ref=cnt.at[q], dst_ref=rcnt.at[d - 1], send_sem=s_cnt.at[d - 1],
            recv_sem=r_cnt.at[d - 1], device_id={"tm": q}, device_id_type=MESH)

    def sort(c):
        for k in range(chunks):
            rows_in(c, k).wait()
            for n in range(tm):
                sl = slice(n * w, (n + 1) * w)
                y = jnp.dot(perm[k], X[c, k * CHUNK:(k + 1) * CHUNK, sl], preferred_element_type=F32)
                Xs[c, k * tiles:(k + 1) * tiles, :, sl] = y[:CHUNK].astype(BF16).reshape(tiles, TILE, w)
                some = y[CHUNK:]
                if k > 0:
                    some = some + sums[n]
                if k < chunks - 1:
                    sums[n] = some
                else:
                    for q in range(tm):
                        ssend[q, c, n * own_rows:(n + 1) * own_rows, :] = some[q * own_rows:(q + 1) * own_rows]

        @pl.when(c == 0)
        def _():
            pl.semaphore_wait(barrier, tm - 1 + space - 1)
            every(tm, lambda d: cnt_copy(d).start(), 1)

        every(tm, lambda d: sum_copy(c, d).start(), 1)

    every(comp, sort)
    for cp in plan_copies:
        cp.wait()

    def mj_copy(d, q):
        at = pl.ds(pl.multiple_of(q * 8, 8), 8)
        return pltpu.make_async_remote_copy(
            src_ref=mj.at[at], dst_ref=mj.at[at], send_sem=s_mj.at[d - 1], recv_sem=r_mj.at[d - 1],
            device_id={"tm": lax.rem(me_t + d, tm)}, device_id_type=MESH)

    ocopy = pltpu.make_async_copy(meanv, mean_out, osem)

    def means():
        for d in range(1, tm):
            cnt_copy(d).wait()
            for c in range(comp):
                sum_copy(c, d).wait()
        total_cnt = cnt[me_t]
        for d in range(tm - 1):
            total_cnt = total_cnt + rcnt[d]
        for c in range(comp):
            tot = ssend[me_t, c]
            for d in range(tm - 1):
                tot = tot + rsum[d, c]
            m = tot / total_cnt[:, 0:1]
            for n in range(tm):
                mine = m[n * own_rows:(n + 1) * own_rows]
                meanv[c, :, n * w:(n + 1) * w] = mine.astype(BF16)
                mean[c, :, n * w:(n + 1) * w] = jnp.concatenate(
                    [mine, jnp.zeros((bins - own_rows, w), F32)], 0).astype(BF16)
        ocopy.start()
        at = [owns[0, me_t * own_rows + i] for i in range(own_rows)]
        tall = (own_rows * nm, bins)

        p = jnp.zeros(tall, F32)
        for c in range(comp):
            p += lax.dot_general(
                jnp.concatenate([mo[c, a] for a in at], 0), mean[c], NT, preferred_element_type=F32)
        flat = jnp.zeros((nm, bins), F32)
        for i in range(own_rows):
            flat = flat + jnp.where(iota((nm, bins), 1) == i, p[i * nm:(i + 1) * nm], 0.0)
        mine = flat.T[:own_rows]
        mj[pl.ds(pl.multiple_of(me_t * 8, 8), 8)] = jnp.concatenate(
            [mine, jnp.zeros((8 - own_rows, nm), F32)], 0)
        for d in range(1, tm):
            mj_copy(d, me_t).start()

    split = pairs - 3

    def project(p):
        prod = jnp.zeros((slots, 2 * nm), F32)
        for c in range(comp):
            sorted_rows = jnp.concatenate([Xs[c, tables[2 * p, s]] for s in range(slots // TILE)], 0)
            prod += lax.dot_general(
                sorted_rows, mo[c, pl.ds(2 * p, 2)].reshape(2 * nm, cells), NT, preferred_element_type=F32)
        for b in range(2):
            prods[pl.ds(pl.multiple_of((2 * p + b) * slots, TILE), slots)] = prod[:, b * nm:(b + 1) * nm]

    def early(i):
        every(4, lambda b: fetch(4 * i + b).wait())
        project(2 * i)
        project(2 * i + 1)

    def late(p):
        @pl.when(p < split)
        def _():
            fetch(2 * p).wait()
            fetch(2 * p + 1).wait()

        @pl.when(p == split)
        def _():
            every(bins, lambda b: fetch(b).wait(), 2 * split)
            means()

        project(p)

    every(split // 2, early)
    every(pairs, late, 2 * (split // 2))

    def mj_done(d):
        mj_copy(d, me_t).wait_send()
        mj_copy(d, lax.rem(me_t + tm - d, tm)).wait_recv()

    every(tm, mj_done, 1)
    rest = mj[...]
    for i in range(3):
        term = rest.astype(BF16)
        rest = rest - term.astype(F32)
        terms[i] = term

    def part_rows(s, h):
        return pl.ds(pl.multiple_of(s * blk + h * part, TILE), part)

    def rs_copy(h, d):
        return pltpu.make_async_remote_copy(
            src_ref=sendc.at[h, d], dst_ref=rsc.at[h, d - 1], send_sem=s_rs.at[h, d - 1],
            recv_sem=r_rs.at[h, d - 1], device_id={"space": lax.rem(me_s + d, space)}, device_id_type=MESH)

    def unsort(i):
        h, d = i // space, space - 1 - lax.rem(i, space)
        q = lax.rem(me_s + d, space)

        here = byrow[part_rows(q, h), :mj_rows]
        off = jnp.dot(here, terms[0], preferred_element_type=F32)
        for i in range(1, 3):
            off = off + jnp.dot(here, terms[i], preferred_element_type=F32)
        for r in range(part):
            acc[h, r:r + 1] = prods[pl.ds(keys[0, q * blk + h * part + r], 1)]
        v = acc[h] - off
        acc[h] = v
        sendc[h, d] = v.astype(BF16)

        @pl.when(d > 0)
        def _():
            rs_copy(h, d).start()

    every(HALVES * space, unsort)

    def ag_copy(h, d, s):
        return pltpu.make_async_remote_copy(
            src_ref=agc.at[h], dst_ref=coef_out.at[part_rows(s, h)], send_sem=s_ag.at[h, d - 1],
            recv_sem=r_ag.at[h, d - 1], device_id={"space": lax.rem(me_s + d, space)}, device_id_type=MESH)

    def keep(h):
        return pltpu.make_async_copy(agc.at[h], coef_out.at[part_rows(me_s, h)], osem_c.at[h])

    def gather(h):
        def add(d, tot):
            rs_copy(h, d).wait()
            return tot + rsc[h, d - 1].astype(F32)

        agc[h] = lax.fori_loop(1, space, add, acc[h]).astype(BF16)
        every(space, lambda d: ag_copy(h, d, me_s).start(), 1)
        keep(h).start()

    every(HALVES, gather)
    ocopy.wait()

    def done(i):
        h, d = i // (space - 1), i % (space - 1) + 1
        ag_copy(h, d, me_s).wait_send()
        ag_copy(h, d, lax.rem(me_s + space - d, space)).wait_recv()

    every(HALVES * (space - 1), done)
    every(HALVES, lambda h: keep(h).wait())


def finish(coef, mean, coef_out, mean_out):
    coef_out[...] = coef[...].astype(F32)
    mean_out[...] = mean[...]


def on_device(snaps, phase_bin, owner_order, modes):
    rows, comp, cells = snaps.shape
    bins, nm = modes.shape[0], modes.shape[1]
    tm, space = lax.axis_size("tm"), lax.axis_size("space")
    blk, w, own_rows = rows // space, cells // tm, bins // tm
    chunks, slots = rows // CHUNK, slots_of(rows)
    ownrow = owner_order.reshape(1, bins)
    vm = pl.BlockSpec(memory_space=pltpu.VMEM)
    hbm = pl.BlockSpec(memory_space=pl.ANY)
    dma = pltpu.SemaphoreType.DMA
    binrow = phase_bin.reshape(1, rows)
    coef, mean = pl.pallas_call(
        functools.partial(kernel, tm, space),
        out_shape=(
            jax.ShapeDtypeStruct((rows, nm), BF16),
            jax.ShapeDtypeStruct((comp, own_rows, cells), BF16),
        ),
        in_specs=[hbm, hbm, hbm, hbm],
        out_specs=(hbm, hbm),
        scratch_shapes=[
            pltpu.VMEM((1, rows), I32),
            pltpu.VMEM((1, bins), I32),
            pltpu.SMEM((1, bins), I32),
            pltpu.VMEM((bins, 128), I32),
            pltpu.SMEM((bins, 128), I32),
            pltpu.VMEM((1, rows), I32),
            pltpu.SMEM((1, rows), I32),
            pltpu.VMEM((comp, own_rows, cells), BF16),
            pltpu.VMEM((comp, rows, cells), BF16),
            pltpu.VMEM((comp, rows // TILE, TILE, cells), BF16),
            pltpu.VMEM((comp, bins, nm, cells), BF16),
            pltpu.VMEM((chunks, CHUNK + bins, CHUNK), BF16),
            pltpu.VMEM((bins * slots, nm), F32),
            pltpu.VMEM((tm, bins, w), F32),
            pltpu.VMEM((tm, comp, bins, w), F32),
            pltpu.VMEM((tm - 1, comp, bins, w), F32),
            pltpu.VMEM((tm, bins, 128), F32),
            pltpu.VMEM((tm - 1, bins, 128), F32),
            pltpu.VMEM((comp, bins, cells), BF16),
            pltpu.VMEM((tm * 8, nm), F32),
            pltpu.VMEM((rows, 128), BF16),
            pltpu.VMEM((3, 8 * tm, nm), BF16),
            pltpu.VMEM((HALVES, blk // HALVES, nm), F32),
            pltpu.VMEM((HALVES, space, blk // HALVES, nm), BF16),
            pltpu.VMEM((HALVES, space - 1, blk // HALVES, nm), BF16),
            pltpu.VMEM((HALVES, blk // HALVES, nm), BF16),
            dma((5,)), dma(()), dma((HALVES,)), dma((comp, chunks)), dma((bins,)),
            dma((tm - 1, comp)), dma((tm - 1, comp)), dma((tm - 1,)), dma((tm - 1,)), dma((tm - 1,)), dma((tm - 1,)),
            dma((HALVES, space - 1)), dma((HALVES, space - 1)), dma((HALVES, space - 1)), dma((HALVES, space - 1)),
        ],
        compiler_params=pltpu.CompilerParams(
            collective_id=0, has_side_effects=True, vmem_limit_bytes=61 * 1024 * 1024
        ),
        cost_estimate=pl.CostEstimate(
            flops=2 * slots * bins * nm * comp * cells,
            bytes_accessed=2 * comp * cells * (rows + bins * nm), transcendentals=0),
    )(binrow, ownrow, snaps.transpose(1, 0, 2), modes.transpose(0, 2, 1, 3))
    coef, mean = pl.pallas_call(
        finish,
        out_shape=(
            jax.ShapeDtypeStruct((rows, nm), F32),
            jax.ShapeDtypeStruct((comp, own_rows, cells), BF16),
        ),
        in_specs=[vm, vm],
        out_specs=(vm, vm),
    )(coef, mean)
    return mean.transpose(1, 0, 2), coef


def solution(mesh):
    in_specs = (P("tm", None, "space"), P("tm"), P(), P(None, None, None, "space"))
    out_specs = (P("tm", None, "space"), P("tm", None))
    return jax.shard_map(
        on_device, mesh=mesh, in_specs=in_specs, out_specs=out_specs, check_vma=False
    )
```

```python
import functools

import jax
import jax.numpy as jnp
from jax import lax
from jax.experimental import pallas as pl
from jax.experimental.pallas import tpu as pltpu
from jax.sharding import PartitionSpec as P

MESH = pl.DeviceIdType.MESH
F32 = jnp.float32
BF16 = jnp.bfloat16
I32 = jnp.int32
NT = (((1,), (1,)), ((), ()))
CHUNK = 256
TILE = 16
HALVES = 2
CAP = 128


def slots_of(rows):
    chunks = rows // CHUNK
    return TILE * ((2 * CAP + (TILE - 2) * chunks) // TILE + chunks)


def iota(shape, dim):
    return lax.broadcasted_iota(I32, shape, dim)


def ones_where(cond):
    return jnp.where(cond, 1.0, 0.0)


def owners(ownrow, rank_of_row):
    bins = ownrow.shape[1]
    return jnp.sum(jnp.where(rank_of_row == iota((bins, bins), 1), ownrow, 0), axis=1, keepdims=True)


def sums_before(x, dim, length):
    total, at, step = x, iota(x.shape, dim) % length, 1
    while step < length:
        total = total + jnp.where(at >= step, pltpu.roll(total, step, dim), 0)
        step *= 2
    return total - x


def kernel(
    tm, space, bins_in, owners_in, snaps, modes, coef_out, mean_out,
    binv, ownv, owns, tablev, tables, keyv, keys, meanv, X, Xs, mo, perm, prods, sums, ssend, rsum, cnt, rcnt, mean, mj,
    byrow, terms, acc, sendc, rsc, agc,
    vsem, osem, osem_c, xsem, msem, s_sum, r_sum, s_cnt, r_cnt, s_mj, r_mj, s_rs, r_rs, s_ag, r_ag,
):
    comp, rows, cells = snaps.shape
    bins, nm = modes.shape[0], modes.shape[2]
    pairs, chunks, tiles = bins // 2, rows // CHUNK, CHUNK // TILE
    slots = slots_of(rows)
    own_rows = bins // tm
    w = cells // tm
    blk = rows // space
    part = blk // HALVES
    mj_rows = 8 * tm
    me_t = lax.axis_index("tm")
    me_s = lax.axis_index("space")

    def every(n, f, first=0):
        lax.fori_loop(first, n, lambda i, _: (f(i), 0)[1], 0)

    first_copies = [
        pltpu.make_async_copy(bins_in, binv, vsem.at[0]), pltpu.make_async_copy(owners_in, ownv, vsem.at[1]),
        pltpu.make_async_copy(owners_in, owns, vsem.at[2])]
    for cp in first_copies:
        cp.start()

    def rows_in(c, k):
        sl = pl.ds(pl.multiple_of(k * CHUNK, CHUNK), CHUNK)
        return pltpu.make_async_copy(snaps.at[c, sl], X.at[c, sl], xsem.at[c, k])

    every(comp * chunks, lambda i: rows_in(i // chunks, i % chunks).start())

    def fetch(b):
        return pltpu.make_async_copy(modes.at[b], mo.at[:, b], msem.at[b])

    every(bins, lambda b: fetch(b).start())

    barrier = pltpu.get_barrier_semaphore()
    for d in range(1, tm):
        pl.semaphore_signal(barrier, inc=1, device_id={"tm": lax.rem(me_t + d, tm)}, device_id_type=MESH)
    for d in range(1, space):
        pl.semaphore_signal(barrier, inc=1, device_id={"space": lax.rem(me_s + d, space)}, device_id_type=MESH)

    for cp in first_copies:
        cp.wait()
    binrow = binv[...]
    ownrow = ownv[...]

    groups = chunks * bins
    hot = jnp.concatenate(
        [jnp.where(binrow[:, k * CHUNK:(k + 1) * CHUNK] == iota((bins, CHUNK), 0), 1, 0) for k in range(chunks)], 0)
    rank = sums_before(hot, 1, CHUNK)
    count = jnp.broadcast_to(jnp.sum(hot, axis=1, keepdims=True), (groups, 128))
    base = sums_before(count, 0, bins)
    even = iota((groups, 128), 0) % 2 == 0
    pair_base = jnp.where(even, base, pltpu.roll(base, 1, 0))
    pair_count = count + jnp.where(even, pltpu.roll(count, groups - 1, 0), pltpu.roll(count, 1, 0))
    first = pair_base // TILE
    n_tiles = jnp.where(pair_count > 0, (pair_base + pair_count - 1) // TILE - first + 1, 0)
    place = iota((bins, 128), 1)
    skip = jnp.zeros((bins, 128), I32)
    table = jnp.zeros((bins, 128), I32)
    own = owners(ownrow, iota((bins, bins), 0))
    j = iota((bins, CHUNK), 0)
    mj_row = 8 * (j // own_rows) + j % own_rows
    for k in range(chunks):
        sl, here = slice(k * CHUNK, (k + 1) * CHUNK), slice(k * bins, (k + 1) * bins)
        bk, f, nk = binrow[:, sl], first[here], n_tiles[here]
        table = table + jnp.where((place >= skip) & (place < skip + nk), tiles * k + f + place - skip, 0)
        slot = jnp.sum(hot[here] * (base[here][:, 0:1] + rank[here]), axis=0, keepdims=True)
        shift = jnp.sum(hot[here] * (TILE * (skip - f))[:, 0:1], axis=0, keepdims=True)
        keyv[:, sl] = slot + shift + bk * slots
        perm[k, :CHUNK, :] = ones_where(slot == iota((CHUNK, CHUNK), 0)).astype(BF16)
        by_owner = bk == own
        perm[k, CHUNK:, :] = ones_where(by_owner).astype(BF16)
        mean_row = jnp.sum(jnp.where(by_owner, mj_row, 0), axis=0, keepdims=True)
        for g in range(CHUNK // 128):
            at_row = jnp.broadcast_to(mean_row[:, g * 128:(g + 1) * 128], (128, 128)).T
            byrow[k * CHUNK + g * 128:k * CHUNK + (g + 1) * 128, :] = ones_where(
                iota((128, 128), 1) == at_row).astype(BF16)
        skip = skip + nk
    tablev[...] = table
    plan_copies = [pltpu.make_async_copy(tablev, tables, vsem.at[3]), pltpu.make_async_copy(keyv, keys, vsem.at[4])]
    for cp in plan_copies:
        cp.start()
    for q in range(tm):
        mine = owners(ownrow, q * own_rows + iota((bins, bins), 0) % own_rows)
        cnt[q] = jnp.broadcast_to(
            jnp.sum(ones_where(mine == binrow), axis=1, keepdims=True), (bins, 128))
    def sum_copy(c, d):
        q = lax.rem(me_t + d, tm)
        return pltpu.make_async_remote_copy(
            src_ref=ssend.at[q, c], dst_ref=rsum.at[d - 1, c], send_sem=s_sum.at[d - 1, c],
            recv_sem=r_sum.at[d - 1, c], device_id={"tm": q}, device_id_type=MESH)

    def cnt_copy(d):
        q = lax.rem(me_t + d, tm)
        return pltpu.make_async_remote_copy(
            src_ref=cnt.at[q], dst_ref=rcnt.at[d - 1], send_sem=s_cnt.at[d - 1],
            recv_sem=r_cnt.at[d - 1], device_id={"tm": q}, device_id_type=MESH)

    def sort(c):
        for k in range(chunks):
            rows_in(c, k).wait()
            for n in range(tm):
                sl = slice(n * w, (n + 1) * w)
                y = jnp.dot(perm[k], X[c, k * CHUNK:(k + 1) * CHUNK, sl], preferred_element_type=F32)
                Xs[c, k * tiles:(k + 1) * tiles, :, sl] = y[:CHUNK].astype(BF16).reshape(tiles, TILE, w)
                some = y[CHUNK:]
                if k > 0:
                    some = some + sums[n]
                if k < chunks - 1:
                    sums[n] = some
                else:
                    for q in range(tm):
                        ssend[q, c, n * own_rows:(n + 1) * own_rows, :] = some[q * own_rows:(q + 1) * own_rows]

        @pl.when(c == 0)
        def _():
            pl.semaphore_wait(barrier, tm - 1 + space - 1)
            every(tm, lambda d: cnt_copy(d).start(), 1)

        every(tm, lambda d: sum_copy(c, d).start(), 1)

    every(comp, sort)
    for cp in plan_copies:
        cp.wait()

    def mj_copy(d, q):
        at = pl.ds(pl.multiple_of(q * 8, 8), 8)
        return pltpu.make_async_remote_copy(
            src_ref=mj.at[at], dst_ref=mj.at[at], send_sem=s_mj.at[d - 1], recv_sem=r_mj.at[d - 1],
            device_id={"tm": lax.rem(me_t + d, tm)}, device_id_type=MESH)

    ocopy = pltpu.make_async_copy(meanv, mean_out, osem)

    def means():
        for d in range(1, tm):
            cnt_copy(d).wait()
            for c in range(comp):
                sum_copy(c, d).wait()
        total_cnt = cnt[me_t]
        for d in range(tm - 1):
            total_cnt = total_cnt + rcnt[d]
        for c in range(comp):
            tot = ssend[me_t, c]
            for d in range(tm - 1):
                tot = tot + rsum[d, c]
            m = tot / total_cnt[:, 0:1]
            for n in range(tm):
                mine = m[n * own_rows:(n + 1) * own_rows]
                meanv[c, :, n * w:(n + 1) * w] = mine.astype(BF16)
                mean[c, :, n * w:(n + 1) * w] = jnp.concatenate(
                    [mine, jnp.zeros((bins - own_rows, w), F32)], 0).astype(BF16)
        ocopy.start()
        at = [owns[0, me_t * own_rows + i] for i in range(own_rows)]
        tall = (own_rows * nm, bins)

        lhs = jnp.concatenate([jnp.concatenate([mo[c, a] for a in at], 0) for c in range(comp)], 1)
        rhs = jnp.concatenate([mean[c] for c in range(comp)], 1)
        p = lax.dot_general(lhs, rhs, NT, preferred_element_type=F32)
        flat = jnp.zeros((nm, bins), F32)
        for i in range(own_rows):
            flat = flat + jnp.where(iota((nm, bins), 1) == i, p[i * nm:(i + 1) * nm], 0.0)
        mine = flat.T[:own_rows]
        mj[pl.ds(pl.multiple_of(me_t * 8, 8), 8)] = jnp.concatenate(
            [mine, jnp.zeros((8 - own_rows, nm), F32)], 0)
        for d in range(1, tm):
            mj_copy(d, me_t).start()

    split = pairs - 3

    def project(p):
        @pl.when(p < split)
        def _():
            fetch(2 * p).wait()
            fetch(2 * p + 1).wait()

        @pl.when(p == split)
        def _():
            every(bins, lambda b: fetch(b).wait(), 2 * split)
            means()

        prod = jnp.zeros((slots, 2 * nm), F32)
        for c in range(comp):
            sorted_rows = jnp.concatenate([Xs[c, tables[2 * p, s]] for s in range(slots // TILE)], 0)
            prod += lax.dot_general(
                sorted_rows, mo[c, pl.ds(2 * p, 2)].reshape(2 * nm, cells), NT, preferred_element_type=F32)
        for b in range(2):
            prods[pl.ds(pl.multiple_of((2 * p + b) * slots, TILE), slots)] = prod[:, b * nm:(b + 1) * nm]

    every(pairs, project)

    def mj_done(d):
        mj_copy(d, me_t).wait_send()
        mj_copy(d, lax.rem(me_t + tm - d, tm)).wait_recv()

    every(tm, mj_done, 1)
    rest = mj[...]
    for i in range(3):
        term = rest.astype(BF16)
        rest = rest - term.astype(F32)
        terms[i] = term

    def part_rows(s, h):
        return pl.ds(pl.multiple_of(s * blk + h * part, TILE), part)

    def rs_copy(h, d):
        return pltpu.make_async_remote_copy(
            src_ref=sendc.at[h, d], dst_ref=rsc.at[h, d - 1], send_sem=s_rs.at[h, d - 1],
            recv_sem=r_rs.at[h, d - 1], device_id={"space": lax.rem(me_s + d, space)}, device_id_type=MESH)

    def unsort(i):
        h, d = i // space, lax.rem(i + 1, space)
        q = lax.rem(me_s + d, space)

        here = byrow[part_rows(q, h), :mj_rows]
        off = jnp.dot(here, terms[0], preferred_element_type=F32)
        for i in range(1, 3):
            off = off + jnp.dot(here, terms[i], preferred_element_type=F32)
        for r in range(part):
            acc[h, r:r + 1] = prods[pl.ds(keys[0, q * blk + h * part + r], 1)]
        v = acc[h] - off
        acc[h] = v
        sendc[h, d] = v.astype(BF16)

        @pl.when(d > 0)
        def _():
            rs_copy(h, d).start()

    every(HALVES * space, unsort)

    def ag_copy(h, d, s):
        return pltpu.make_async_remote_copy(
            src_ref=agc.at[h], dst_ref=coef_out.at[part_rows(s, h)], send_sem=s_ag.at[h, d - 1],
            recv_sem=r_ag.at[h, d - 1], device_id={"space": lax.rem(me_s + d, space)}, device_id_type=MESH)

    def keep(h):
        return pltpu.make_async_copy(agc.at[h], coef_out.at[part_rows(me_s, h)], osem_c.at[h])

    def gather(h):
        def add(d, tot):
            rs_copy(h, d).wait()
            return tot + rsc[h, d - 1].astype(F32)

        agc[h] = lax.fori_loop(1, space, add, acc[h]).astype(BF16)
        every(space, lambda d: ag_copy(h, d, me_s).start(), 1)
        keep(h).start()

    every(HALVES, gather)
    ocopy.wait()

    def done(i):
        h, d = i // (space - 1), i % (space - 1) + 1
        ag_copy(h, d, me_s).wait_send()
        ag_copy(h, d, lax.rem(me_s + space - d, space)).wait_recv()

    every(HALVES * (space - 1), done)
    every(HALVES, lambda h: keep(h).wait())


def finish(coef, mean, coef_out, mean_out):
    coef_out[...] = coef[...].astype(F32)
    mean_out[...] = mean[...]


def on_device(snaps, phase_bin, owner_order, modes):
    rows, comp, cells = snaps.shape
    bins, nm = modes.shape[0], modes.shape[1]
    tm, space = lax.axis_size("tm"), lax.axis_size("space")
    blk, w, own_rows = rows // space, cells // tm, bins // tm
    chunks, slots = rows // CHUNK, slots_of(rows)
    ownrow = owner_order.reshape(1, bins)
    vm = pl.BlockSpec(memory_space=pltpu.VMEM)
    hbm = pl.BlockSpec(memory_space=pl.ANY)
    dma = pltpu.SemaphoreType.DMA
    binrow = phase_bin.reshape(1, rows)
    coef, mean = pl.pallas_call(
        functools.partial(kernel, tm, space),
        out_shape=(
            jax.ShapeDtypeStruct((rows, nm), BF16),
            jax.ShapeDtypeStruct((comp, own_rows, cells), BF16),
        ),
        in_specs=[hbm, hbm, hbm, hbm],
        out_specs=(hbm, hbm),
        scratch_shapes=[
            pltpu.VMEM((1, rows), I32),
            pltpu.VMEM((1, bins), I32),
            pltpu.SMEM((1, bins), I32),
            pltpu.VMEM((bins, 128), I32),
            pltpu.SMEM((bins, 128), I32),
            pltpu.VMEM((1, rows), I32),
            pltpu.SMEM((1, rows), I32),
            pltpu.VMEM((comp, own_rows, cells), BF16),
            pltpu.VMEM((comp, rows, cells), BF16),
            pltpu.VMEM((comp, rows // TILE, TILE, cells), BF16),
            pltpu.VMEM((comp, bins, nm, cells), BF16),
            pltpu.VMEM((chunks, CHUNK + bins, CHUNK), BF16),
            pltpu.VMEM((bins * slots, nm), F32),
            pltpu.VMEM((tm, bins, w), F32),
            pltpu.VMEM((tm, comp, bins, w), F32),
            pltpu.VMEM((tm - 1, comp, bins, w), F32),
            pltpu.VMEM((tm, bins, 128), F32),
            pltpu.VMEM((tm - 1, bins, 128), F32),
            pltpu.VMEM((comp, bins, cells), BF16),
            pltpu.VMEM((tm * 8, nm), F32),
            pltpu.VMEM((rows, 128), BF16),
            pltpu.VMEM((3, 8 * tm, nm), BF16),
            pltpu.VMEM((HALVES, blk // HALVES, nm), F32),
            pltpu.VMEM((HALVES, space, blk // HALVES, nm), BF16),
            pltpu.VMEM((HALVES, space - 1, blk // HALVES, nm), BF16),
            pltpu.VMEM((HALVES, blk // HALVES, nm), BF16),
            dma((5,)), dma(()), dma((HALVES,)), dma((comp, chunks)), dma((bins,)),
            dma((tm - 1, comp)), dma((tm - 1, comp)), dma((tm - 1,)), dma((tm - 1,)), dma((tm - 1,)), dma((tm - 1,)),
            dma((HALVES, space - 1)), dma((HALVES, space - 1)), dma((HALVES, space - 1)), dma((HALVES, space - 1)),
        ],
        compiler_params=pltpu.CompilerParams(
            collective_id=0, has_side_effects=True, vmem_limit_bytes=61 * 1024 * 1024
        ),
        cost_estimate=pl.CostEstimate(
            flops=2 * slots * bins * nm * comp * cells,
            bytes_accessed=2 * comp * cells * (rows + bins * nm), transcendentals=0),
    )(binrow, ownrow, snaps.transpose(1, 0, 2), modes.transpose(0, 2, 1, 3))
    coef, mean = pl.pallas_call(
        finish,
        out_shape=(
            jax.ShapeDtypeStruct((rows, nm), F32),
            jax.ShapeDtypeStruct((comp, own_rows, cells), BF16),
        ),
        in_specs=[vm, vm],
        out_specs=(vm, vm),
    )(coef, mean)
    return mean.transpose(1, 0, 2), coef


def solution(mesh):
    in_specs = (P("tm", None, "space"), P("tm"), P(), P(None, None, None, "space"))
    out_specs = (P("tm", None, "space"), P("tm", None))
    return jax.shard_map(
        on_device, mesh=mesh, in_specs=in_specs, out_specs=out_specs, check_vma=False
    )
```
